128 devices in a mesh: row: 8 (over z, core), col: 16 (over x, y).
Axes of the slice: x: 4, y: 4, z: 4, core: 2. Of those that a mesh axis runs over, the one named last changes fastest.
Arguments:
- pair: bfloat16 [2048, 2048, 128], P('row', 'col'), may hold values from -6 to 6
- node_state: bfloat16 [2048, 64], P(('row', 'col')), may hold values from -6 to 6
- coords: float32 [3, 3, 2048], P(None, None, ('row', 'col')), may hold values from -8 to 8
- neighbours: int32 [2048, 64], P('row'), may hold values from 0 to 2047, as said below
- chain: int32 [2048], replicated, may hold values from 0 to 3, never falling along the last dimension, each value on 1 to 1024 neighbouring positions
- w_edge: bfloat16 [128, 64], replicated, may hold values from -0.5 to 0.5
- w_radial: bfloat16 [36, 64], replicated, may hold values from -3 to 3
- w_query: bfloat16 [64, 64], replicated, may hold values from -0.75 to 0.75
- w_keyval: bfloat16 [64, 128], replicated, may hold values from -0.75 to 0.75
- w_edge_kv: bfloat16 [64, 128], replicated, may hold values from -0.75 to 0.75
- w_out: bfloat16 [64, 64], replicated, may hold values from -0.75 to 0.75
- w_move: bfloat16 [64, 12], replicated, may hold values from -0.75 to 0.75
- w_trans_in: bfloat16 [128, 256], replicated, may hold values from -0.5 to 0.5
- w_trans_out: bfloat16 [256, 128], replicated, may hold values from -0.375 to 0.375
- w_gate: bfloat16 [128, 128], replicated, may hold values from -0.5 to 0.5
- w_feat_in: bfloat16 [42, 128], replicated, may hold values from -3 to 3
- w_feat_out: bfloat16 [128, 128], replicated, may hold values from -0.5 to 0.5
Outputs:
- pair_out: bfloat16 [2048, 2048, 128], P('row', 'col')
- node_out: float32 [2048, 64], P(('row', 'col'))
- coords_out: float32 [3, 3, 2048], P(None, None, ('row', 'col'))
The draws below stay inside these ranges and needn't reach their ends.
Inputs may be any that keep to these rules, and one draw needn't show every extreme that they name: Each row lists 64 distinct residues other than the residue itself. Among the neighbours of the 16 residues of one device (residues d * 16 to (d + 1) * 16 - 1), at most 128 lie in one column block of 128 residues, and exactly 128 lie in the column block that holds those residues.
All inputs are finite; a program needn't handle non-finite values.
Results may differ from the reference program's by a relative error of at most 0.0052.
Values may be sent and summed in bfloat16 or wider, within the bound.
No kernel may reach another device: no remote copies, remote signals or barrier semaphores. Data moves between devices by JAX's collectives and lax.ppermute only.
A program may use at most 128 MiB of HBM per device.

```python
import math
import jax
import jax.numpy as jnp
import numpy as np
from jax import lax

C = 128
HID2 = 256
DS = 64
DE = 64
HEADS = 4
K = 64
NRBF = 36
L = 2048
TILE = 128
HOME = 8
NF = 42


def draw_neighbours(key, part):
    key = jax.random.fold_in(key, 11)
    key_tiles = jax.random.fold_in(key, 1)
    key_offsets = jax.random.fold_in(key, 2)
    residue = jnp.arange(L, dtype=jnp.int32)
    home_tile = residue // TILE
    home_start = home_tile * TILE
    half = HOME // 2
    window = jnp.concatenate([jnp.arange(-half, 0, dtype=jnp.int32), jnp.arange(1, half + 1, dtype=jnp.int32)])
    window_nbrs = home_start[:, None] + jnp.mod(residue[:, None] - home_start[:, None] + window[None, :], TILE)
    tile_count = L // TILE
    slot_total = (tile_count - 1) * HOME
    scores = jax.random.randint(key_tiles, (L, slot_total), 0, 1 << 20) * slot_total + jnp.arange(slot_total, dtype=jnp.int32)[None, :]
    top_vals, chosen = lax.top_k(scores, K - HOME)
    chosen = chosen.astype(jnp.int32)
    far_block = chosen // HOME
    far_tiles = jnp.mod(home_tile[:, None] + 1 + far_block, tile_count)
    offset_scores = jax.random.randint(key_offsets, (L, tile_count - 1, TILE), 0, 1 << 20) * TILE + jnp.arange(TILE, dtype=jnp.int32)[None, None, :]
    top_offs, far_offsets = lax.top_k(offset_scores, HOME)
    far_offsets = far_offsets.astype(jnp.int32).reshape(L, slot_total)
    picked_offsets = jnp.take_along_axis(far_offsets, chosen, axis=1)
    far_nbrs = far_tiles * TILE + picked_offsets
    return jnp.concatenate([window_nbrs, far_nbrs], axis=1).astype(jnp.int32)


def levels(stream_key, shape, pieces, least, top_value):
    def one(dim, parts):
        heights = jax.random.uniform(jax.random.fold_in(jax.random.fold_in(stream_key, 6), dim), (parts,), jnp.float32, least / len(pieces), top_value / len(pieces))
        return jnp.repeat(jnp.exp(heights), shape[dim] // parts).reshape((-1,) + (1,) * (len(shape) - dim - 1))

    gain = one(*pieces[0])
    for cut in pieces[1:]:
        gain = gain * one(*cut)
    return gain


def profile(number_of, total, limit, skew):
    portions = [(1 << 20) // math.isqrt(standing ** skew) + 1 for standing in range(2, number_of + 1)]
    spare, holding = total - limit - (number_of - 1), [1] * (number_of - 1)
    while spare > 0:
        movable = [i for i in range(number_of - 1) if holding[i] < limit]
        whole, left = sum([portions[i] for i in movable]), spare
        for i in movable:
            extra = min(limit - holding[i], max(1, left * portions[i] // whole), spare)
            holding[i] = holding[i] + extra
            spare = spare - extra
    return np.array([limit] + holding)


def uneven_parts(own_key, count, total, reach, slope):
    if count == 2:
        one = jax.random.randint(own_key, (), max(1, total - reach), min(reach, total - 1) + 1)
        return jnp.stack([one, total - one])
    lengths = jnp.asarray(profile(count, total, reach, slope), jnp.int32)
    pairs = (count - 1) // 2
    donor, sink = lengths[1:1 + 2 * pairs:2], lengths[2:2 + 2 * pairs:2]
    margin = jnp.minimum(donor - 1, reach - sink)
    shifted = jax.random.randint(jax.random.fold_in(own_key, 1), (pairs,), 0, 1 << 20) % (margin + 1)
    lengths = lengths.at[1:1 + 2 * pairs:2].set(donor - shifted).at[2:2 + 2 * pairs:2].set(sink + shifted)
    return lengths[jax.random.permutation(jax.random.fold_in(own_key, 2), count)]


def gaussian(key, extent, deviation, most, pieces=(), kind=jnp.bfloat16):
    gain = levels(key, extent, pieces, -0.22, 0.18) if pieces else 1.0
    result = jax.random.normal(key, extent, jnp.float32) * deviation * gain
    return jnp.minimum(jnp.maximum(result, -most), most).astype(kind)


def setup_inputs(seed: int = 0) -> dict:
    streams_of = jax.random.split(jax.random.key(seed), 18)
    return {
        "pair": gaussian(streams_of[0], (L, L, C), 1.0, 6.0, ((0, 8), (1, 16))),
        "node_state": gaussian(streams_of[1], (L, DS), 1.0, 6.0, ((0, 128),)),
        "coords": gaussian(streams_of[2], (3, 3, L), 2.0, 8.0, ((2, 128),), jnp.float32),
        "neighbours": draw_neighbours(jax.random.fold_in(streams_of[17], 71), 0),
        "chain": jnp.searchsorted(jnp.cumsum(uneven_parts(streams_of[4], 4, L, L // 2, 1)), jnp.arange(L), side="right").astype(jnp.int32),
        "w_edge": gaussian(streams_of[5], (C, DE), C ** -0.5, 0.5),
        "w_radial": gaussian(streams_of[6], (NRBF, DE), 4 ** -0.5, 3.0),
        "w_query": gaussian(streams_of[7], (DS, DS), DS ** -0.5, 0.75),
        "w_keyval": gaussian(streams_of[8], (DS, 2 * DS), DS ** -0.5, 0.75),
        "w_edge_kv": gaussian(streams_of[9], (DE, 2 * DS), DE ** -0.5, 0.75),
        "w_out": gaussian(streams_of[10], (DS, DS), DS ** -0.5, 0.75),
        "w_move": gaussian(streams_of[11], (DE, 3 * HEADS), DE ** -0.5, 0.75),
        "w_trans_in": gaussian(streams_of[12], (C, HID2), C ** -0.5, 0.5),
        "w_trans_out": gaussian(streams_of[13], (HID2, C), HID2 ** -0.5, 0.375),
        "w_gate": gaussian(streams_of[14], (C, C), C ** -0.5, 0.5),
        "w_feat_in": gaussian(streams_of[15], (NF, C), 4 ** -0.5, 3.0),
        "w_feat_out": gaussian(streams_of[16], (C, C), C ** -0.5, 0.5),
    }


dist_top = 12.0
basis_width = 0.5
block_rows = 64

def radial_basis(distance):
    centres = jnp.arange(NRBF, dtype=jnp.float32) * (dist_top / (NRBF - 1))
    centres = centres.reshape((NRBF,) + (1,) * distance.ndim)
    return jnp.exp(-jnp.square((distance[None] - centres) / basis_width))

def edge_layer(edge_in, flat_lists, states, coords_own, keyval_all, coords_all, w_edge, w_radial, w_query, w_edge_kv, w_out, w_move):
    channels_node = states.shape[1]
    head_count = HEADS
    head_size = channels_node // head_count
    own_count = states.shape[0]
    edge_count = flat_lists.shape[0]
    nearby = coords_all[:, :, flat_lists]
    relative = nearby - jnp.repeat(coords_own, K, axis=2)
    distance = jnp.sqrt(lax.optimization_barrier(jnp.sum(relative[1] * relative[1], axis=0)))
    edge_basis = radial_basis(distance).astype(jnp.bfloat16)
    pre_act = jnp.dot(edge_in, w_edge, preferred_element_type=jnp.float32)
    pre_act = pre_act + lax.dot_general(edge_basis, w_radial, (((0,), (0,)), ((), ())), preferred_element_type=jnp.float32)
    edge_hidden = jax.nn.silu(pre_act).astype(jnp.bfloat16)
    edge_mix = jnp.dot(edge_hidden, w_edge_kv, preferred_element_type=jnp.float32)
    picked = keyval_all[flat_lists].astype(jnp.float32)
    key_part = picked[:, :channels_node] + edge_mix[:, :channels_node]
    values = picked[:, channels_node:] + edge_mix[:, channels_node:]
    queries = jnp.repeat(jnp.dot(states, w_query, preferred_element_type=jnp.float32), K, axis=0)
    logits = lax.optimization_barrier(jnp.sum((queries * key_part).reshape(edge_count, head_count, head_size), axis=2)) / math.sqrt(head_size)
    attention = jax.nn.sigmoid(logits)
    weighted = (attention[:, :, None] * values.reshape(edge_count, head_count, head_size)).reshape(own_count, K, channels_node)
    message = (lax.optimization_barrier(jnp.sum(weighted, axis=1)) / K).astype(jnp.bfloat16)
    node_out = states.astype(jnp.float32) + jnp.dot(message, w_out, preferred_element_type=jnp.float32)
    moves_raw = jnp.dot(edge_hidden, w_move, preferred_element_type=jnp.float32).reshape(edge_count, 3, head_count)
    move_coef = lax.optimization_barrier(jnp.sum(moves_raw * attention[:, None, :], axis=2)) / K
    coord_shift = lax.optimization_barrier(jnp.sum((jnp.transpose(move_coef)[:, None, :] * relative).reshape(3, 3, own_count, K), axis=3))
    return (node_out, coords_own + coord_shift)

def pair_features(row_x, col_x, row_chain, col_chain, row_pos, col_pos):
    alpha_row = row_x[1]
    alpha_col = col_x[1]
    displace = alpha_col[:, None, :] - alpha_row[:, :, None]
    distance = jnp.sqrt(lax.optimization_barrier(jnp.sum(displace * displace, axis=0)))
    inverse = 1.0 / (1.0 + distance)
    bond_rn = row_x[0] - alpha_row
    bond_rc = row_x[2] - alpha_row
    bond_cn = col_x[0] - alpha_col
    bond_cc = col_x[2] - alpha_col
    orient_rn = lax.optimization_barrier(jnp.sum(bond_rn[:, :, None] * displace, axis=0)) * inverse
    orient_rc = lax.optimization_barrier(jnp.sum(bond_rc[:, :, None] * displace, axis=0)) * inverse
    orient_cn = -lax.optimization_barrier(jnp.sum(bond_cn[:, None, :] * displace, axis=0)) * inverse
    orient_cc = -lax.optimization_barrier(jnp.sum(bond_cc[:, None, :] * displace, axis=0)) * inverse
    same_chain = (row_chain[:, None] == col_chain[None, :]).astype(jnp.float32)
    offset = same_chain * jnp.clip(col_pos[None, :] - row_pos[:, None], -32, 32).astype(jnp.float32) / 32.0
    tail_feats = jnp.stack([orient_rn, orient_rc, orient_cn, orient_cc, same_chain, offset], axis=0)
    return jnp.concatenate([radial_basis(distance), tail_feats], axis=0).astype(jnp.bfloat16)

def pair_update(pair_block, features, w_trans_in, w_trans_out, w_gate, w_feat_in, w_feat_out):
    row_count, col_width, channels = pair_block.shape
    flat_pair = pair_block.reshape(-1, channels).astype(jnp.float32)
    row_mean = lax.optimization_barrier(jnp.mean(flat_pair, axis=1, keepdims=True))
    centred = flat_pair - row_mean
    normed = (centred * lax.rsqrt(lax.optimization_barrier(jnp.mean(centred * centred, axis=1, keepdims=True)) + 1e-05)).astype(jnp.bfloat16)
    trans_hidden = jax.nn.relu(jnp.dot(normed, w_trans_in, preferred_element_type=jnp.float32)).astype(jnp.bfloat16)
    trans_out = jnp.dot(trans_hidden, w_trans_out, preferred_element_type=jnp.float32)
    gate_val = jax.nn.sigmoid(jnp.dot(normed, w_gate, preferred_element_type=jnp.float32))
    feat_pre = lax.dot_general(features.reshape(features.shape[0], -1), w_feat_in, (((0,), (0,)), ((), ())), preferred_element_type=jnp.float32)
    feat_hidden = jax.nn.silu(feat_pre).astype(jnp.bfloat16)
    struct_term = jnp.dot(feat_hidden, w_feat_out, preferred_element_type=jnp.float32)
    return (flat_pair + trans_out + gate_val * struct_term).astype(jnp.bfloat16).reshape(row_count, col_width, channels)

def reference(pair, node_state, coords, neighbours, chain, w_edge, w_radial, w_query, w_keyval, w_edge_kv, w_out, w_move, w_trans_in, w_trans_out, w_gate, w_feat_in, w_feat_out):
    flat_lists = neighbours.reshape(-1)
    own_rows = jnp.repeat(jnp.arange(L, dtype=jnp.int32), K)
    edge_in = pair.reshape(-1, C)[own_rows * L + flat_lists]
    keyval_all = jnp.dot(node_state, w_keyval, preferred_element_type=jnp.float32).astype(jnp.bfloat16)
    node_out, coords_out = edge_layer(edge_in, flat_lists, node_state, coords, keyval_all, coords, w_edge, w_radial, w_query, w_edge_kv, w_out, w_move)
    positions = jnp.arange(L, dtype=jnp.int32)

    def one_block(row_start):
        pair_block = lax.dynamic_slice_in_dim(pair, row_start, block_rows, 0)
        row_x = lax.dynamic_slice_in_dim(coords_out, row_start, block_rows, 2)
        row_chain = lax.dynamic_slice_in_dim(chain, row_start, block_rows, 0)
        row_pos = row_start + jnp.arange(block_rows, dtype=jnp.int32)
        features = pair_features(row_x, coords_out, row_chain, chain, row_pos, positions)
        return pair_update(pair_block, features, w_trans_in, w_trans_out, w_gate, w_feat_in, w_feat_out)
    starts = jnp.arange(L // block_rows, dtype=jnp.int32) * block_rows
    pair_out = lax.map(one_block, starts).reshape(L, L, C)
    return (pair_out, node_out, coords_out)
```

```python
import functools

import jax
import jax.numpy as jnp
from jax import lax
from jax.experimental import pallas as pl
from jax.experimental.pallas import tpu as pltpu
from jax.sharding import PartitionSpec as P

K = 64
NRBF = 36
BOTH = ("row", "col")
F32 = jnp.float32
BF16 = jnp.bfloat16
CENTRE_STEP = 12.0 / 35.0
PIECES = 64
GROUP = 16
SLOTS = 128
GROUPS_PER_STEP = 4
VMEM_LIMIT = 48 * 1024 * 1024


def iota(shape, dim):
    return lax.broadcasted_iota(jnp.int32, shape, dim)


def dot(a, b):
    return jnp.dot(a, b, preferred_element_type=F32)


def dot_t(a, b):
    return lax.dot_general(a, b, (((0,), (0,)), ((), ())), preferred_element_type=F32)


def dot_nt(a, b):
    return lax.dot_general(a, b, (((1,), (1,)), ((), ())), preferred_element_type=F32)


def split2(v):
    high = v.astype(BF16)
    low = (v - high.astype(F32)).astype(BF16)
    return jnp.concatenate([high, low], axis=1)


def sigmoid(v):
    return 0.5 * jnp.tanh(0.5 * v) + 0.5


def silu(v):
    half = 0.5 * v
    return half + half * jnp.tanh(half)


def record_kernel(node_ref, coords_ref, out_ref, parts_ref):
    parts_ref[...] = jnp.zeros_like(parts_ref)
    for a in range(3):
        value = coords_ref[a]
        high = value.astype(BF16).astype(F32)
        rest = value - high
        mid = rest.astype(BF16).astype(F32)
        parts_ref[pl.ds(PIECES + 3 * a, 3), :] = high
        parts_ref[pl.ds(PIECES + 16 + 3 * a, 3), :] = mid
        parts_ref[pl.ds(PIECES + 32 + 3 * a, 3), :] = rest - mid
    eye = (iota((GROUP, GROUP), 0) == iota((GROUP, GROUP), 1)).astype(F32).astype(BF16)
    widen = (iota((64, 128), 0) == iota((64, 128), 1)).astype(F32).astype(BF16)
    record = dot(node_ref[...], widen) + dot_nt(eye, parts_ref[...].astype(BF16))
    out_ref[...] = jnp.broadcast_to(record.astype(BF16)[None], out_ref.shape)


def records(node_state, coords, copies):
    return pl.pallas_call(
        record_kernel,
        out_shape=jax.ShapeDtypeStruct((copies, GROUP, 128), BF16),
        scratch_shapes=[pltpu.VMEM((128, GROUP), F32)],
        name="records",
    )(node_state, coords)


def select_kernel(place_ref, lists_ref, pair_ref, w_edge_ref, out_ref, where_ref, w_ref):
    @pl.when(pl.program_id(0) == 0)
    def _():
        spot = iota((GROUP * 128, 128), 0)
        lane = iota((GROUP * 128, 128), 1)
        column = (jnp.bitwise_and(spot, 127) + 1).astype(F32)
        residue = (lax.shift_right_logical(spot, 7) + 1).astype(F32)
        where_ref[...] = jnp.where(lane == 64, column, jnp.where(lane == 65, residue, 0.0)).astype(BF16)
        widen = (iota((64, 128), 0) == iota((64, 128), 1)).astype(F32).astype(BF16)
        w_ref[...] = dot(w_edge_ref[...], widen).astype(BF16)

    start = place_ref[1] * 128
    lists = (lists_ref[...] - start).astype(F32)
    lists = jnp.concatenate([lists, jnp.full((GROUP, 64), -1.0, F32)], axis=1)
    by_slot = jnp.transpose(lists)
    column = iota((K, 128), 1).astype(F32)
    rows = []
    for i in range(GROUP):
        hit = by_slot[:K, i : i + 1] == column
        rows.append(jnp.sum(jnp.where(hit, 1.0, 0.0), axis=0, keepdims=True))
    chosen = jnp.concatenate(rows, axis=0)
    chosen_b = chosen.astype(BF16)
    before = (iota((128, 128), 0) < iota((128, 128), 1)).astype(F32).astype(BF16)
    earlier = (iota((GROUP, GROUP), 0) > iota((GROUP, GROUP), 1)).astype(F32).astype(BF16)
    totals = dot(chosen_b, jnp.ones((128, 128), BF16))
    rank = dot(chosen_b, before) + dot(earlier, totals.astype(BF16))
    rank = jnp.where(chosen > 0.0, rank, -1.0)
    slot = iota((SLOTS, 128), 0).astype(F32)
    picks = [jnp.where(slot == rank[i : i + 1, :], 1.0, 0.0).astype(BF16) for i in range(GROUP)]
    pick = jnp.concatenate(picks, axis=1)
    found = dot(pick, pair_ref[...].reshape(GROUP * 128, 128))
    marks = dot(pick, where_ref[...])
    out_ref[...] = dot(found.astype(BF16), w_ref[...]) + marks


def select_edges(place, neighbours, pair, w_edge):
    groups = pair.shape[0] // GROUP
    return pl.pallas_call(
        select_kernel,
        grid_spec=pltpu.PrefetchScalarGridSpec(
            num_scalar_prefetch=1,
            grid=(groups,),
            in_specs=[
                pl.BlockSpec((GROUP, K), lambda g, place: (g, 0)),
                pl.BlockSpec((GROUP, 128, 128), lambda g, place: (g, 0, 0)),
                pl.BlockSpec((128, 64), lambda g, place: (0, 0)),
            ],
            out_specs=pl.BlockSpec((SLOTS, 128), lambda g, place: (g, 0)),
            scratch_shapes=[pltpu.VMEM((GROUP * 128, 128), BF16), pltpu.VMEM((128, 128), BF16)],
        ),
        out_shape=jax.ShapeDtypeStruct((groups * SLOTS, 128), F32),
        compiler_params=pltpu.CompilerParams(vmem_limit_bytes=VMEM_LIMIT),
        cost_estimate=pl.CostEstimate(flops=3_000_000_000, bytes_accessed=9 * 2**20, transcendentals=0),
        name="select_edges",
    )(place, neighbours, pair, w_edge)


def edge_kernel(
    place_ref,
    edges_ref,
    cols_ref,
    rows_ref,
    w_radial_ref,
    w_query_ref,
    w_keyval_ref,
    w_edge_kv_ref,
    w_move_ref,
    out_ref,
    w_keyval_s,
    w_query_s,
    w_radial_s,
    w_mix_s,
):
    for ref in (w_keyval_s, w_query_s, w_radial_s, w_mix_s):
        ref[...] = jnp.zeros_like(ref)
    w_keyval_s[0:64, :] = w_keyval_ref[...]
    w_query_s[0:64, 0:64] = w_query_ref[...]
    w_radial_s[0:36, 0:64] = w_radial_ref[...]
    w_mix_s[0:64, 0:128] = w_edge_kv_ref[...]
    w_mix_s[0:64, 128:140] = w_move_ref[...]
    cols = cols_ref[...]
    keyval = dot(cols, w_keyval_s[...]).astype(BF16)
    by_column = jnp.concatenate([keyval, cols], axis=1)
    lane = iota((1, 128), 1)
    source = iota((256, 256), 0)
    target = iota((256, 256), 1)
    channel = jnp.bitwise_and(source, 127)
    head = lax.shift_right_logical(channel, 4)
    for_value = (target >= 64) & (target < 128) & (lax.shift_right_logical(target - 64, 4) == head)
    for_move = (target >= 128) & (target < 140) & (jnp.bitwise_and(target, 3) == head)
    heads = jnp.where((channel < 64) & (for_value | for_move), 0.125, 0.0).astype(BF16)
    source = jnp.bitwise_and(iota((256, 128), 0), 127)
    target = iota((256, 128), 1) - PIECES
    low_atom = lax.shift_right_logical(source, 2) * 3
    spread = jnp.where(
        (source < 12) & (target >= low_atom) & (target < low_atom + 3), 1.0, 0.0
    ).astype(BF16)
    centre = lane.astype(F32) * CENTRE_STEP
    alpha = jnp.where((lane >= PIECES + 3) & (lane < PIECES + 6), 1.0, 0.0)
    per = GROUPS_PER_STEP * SLOTS
    own = GROUPS_PER_STEP * GROUP
    steps = edges_ref.shape[0] // per
    lane_f = lane.astype(F32)
    shift_by = lax.shift_right_logical(iota((per, 128), 0), 7) * GROUP
    parts = []
    for step in range(steps):
        edges = edges_ref[pl.ds(step * per, per), :]
        column = edges[:, 64:65] - 1.0
        residue = edges[:, 65:66] - 1.0
        pick_col = jnp.where(column == lane_f, 1.0, 0.0).astype(BF16)
        target_row = jnp.where((lane >= shift_by) & (lane < shift_by + GROUP), lane - shift_by, -2).astype(F32)
        pick_row = jnp.where(residue == target_row, 1.0, 0.0).astype(BF16)
        rows = rows_ref[pl.ds(step * own, own), :]
        rows = jnp.concatenate([rows, jnp.zeros((128 - own, 128), BF16)], axis=0)
        from_col = dot(pick_col, by_column)
        from_row = dot(pick_row, rows)
        gap = from_col[:, 128:] - from_row
        relative = gap + pltpu.roll(gap, 112, 1) + pltpu.roll(gap, 96, 1)
        distance = jnp.sqrt(jnp.sum(relative * relative * alpha, axis=1, keepdims=True))
        offset = (distance - centre) * 2.0
        basis = jnp.exp(-(offset * offset)).astype(BF16)
        hidden = silu(edges + dot(basis, w_radial_s[...])).astype(BF16)
        mix = dot(hidden, w_mix_s[...])
        keyval_edge = from_col[:, :128] + mix[:, :128]
        queries = dot(from_row.astype(BF16), w_query_s[...])
        attention = 0.5 * jnp.tanh(dot(split2(queries * keyval_edge), heads)) + 0.5
        values = attention[:, :128] * keyval_edge
        moves = attention[:, 128:] * mix[:, 128:]
        move = dot(split2(moves), spread) * relative
        both = jnp.where(lane < 64, pltpu.roll(move, 64, 1), values)
        summed = dot_t(pick_row, split2(both))
        parts.append((summed[:own, :128] + summed[:own, 128:]) * (1.0 / K))
    total = jnp.concatenate(parts, axis=0)
    atoms = rows_ref[...].astype(F32)
    atoms = atoms + pltpu.roll(atoms, 112, 1) + pltpu.roll(atoms, 96, 1)
    first = jnp.where(place_ref[1] == 0, 1.0, 0.0)
    total = total + jnp.where(lane < 9, pltpu.roll(atoms, 64, 1), 0.0) * first
    by_lane = jnp.transpose(total)
    groups = out_ref.shape[0]
    for d in range(groups):
        out_ref[d, 0:16, :] = total[d * GROUP : (d + 1) * GROUP, :]
        out_ref[d, 16:24, :] = by_lane[0:8, 0:128]
        out_ref[d, 24:32, :] = by_lane[0:8, 128:256]
        out_ref[d, 32:40, :] = jnp.concatenate(
            [by_lane[8:9, 0:128], by_lane[8:9, 128:256], jnp.zeros((6, 128), F32)], axis=0
        )


def edge_sums(place, edges, table, w_radial, w_query, w_keyval, w_edge_kv, w_move):
    groups = edges.shape[0] // SLOTS
    whole = lambda shape: pl.BlockSpec(shape, lambda i, place: (0,) * len(shape))
    return pl.pallas_call(
        edge_kernel,
        grid_spec=pltpu.PrefetchScalarGridSpec(
            num_scalar_prefetch=1,
            grid=(1,),
            in_specs=[
                whole(edges.shape),
                pl.BlockSpec((128, 128), lambda i, place: (place[1], 0)),
                pl.BlockSpec((256, 128), lambda i, place: (place[0], 0)),
                whole(w_radial.shape),
                whole(w_query.shape),
                whole(w_keyval.shape),
                whole(w_edge_kv.shape),
                whole(w_move.shape),
            ],
            out_specs=whole((groups, 40, 128)),
            scratch_shapes=[
                pltpu.VMEM((128, 128), BF16),
                pltpu.VMEM((128, 128), BF16),
                pltpu.VMEM((128, 128), BF16),
                pltpu.VMEM((128, 256), BF16),
            ],
        ),
        out_shape=jax.ShapeDtypeStruct((groups, 40, 128), F32),
        compiler_params=pltpu.CompilerParams(vmem_limit_bytes=VMEM_LIMIT),
        cost_estimate=pl.CostEstimate(flops=2_000_000_000, bytes_accessed=3 * 2**20, transcendentals=0),
        name="edge_sums",
    )(place, edges, table, table, w_radial, w_query, w_keyval, w_edge_kv, w_move)


def total_kernel(place_ref, parts_ref, node_ref, w_out_ref, node_out_ref, own_ref, rows_ref, send_ref, w_ref):
    col = place_ref[1]
    total = parts_ref[0]
    for d in range(1, parts_ref.shape[0]):
        total = total + parts_ref[d]
    w_ref[...] = jnp.zeros_like(w_ref)
    w_ref[64:128, :] = w_out_ref[...]
    message = total[0:16, :].astype(BF16)
    node_out_ref[...] = node_ref[...].astype(F32) + dot(message, w_ref[...])
    left = jnp.concatenate([total[16:24, :], total[32:33, :], jnp.zeros((7, 128), F32)], axis=0)
    right = jnp.concatenate([total[24:32, :], total[33:34, :], jnp.zeros((7, 128), F32)], axis=0)
    rows_ref[:, 0:128] = left
    rows_ref[:, 128:256] = right
    odd = jnp.bitwise_and(col, 1) == 1
    send_ref[...] = jnp.broadcast_to(jnp.where(odd, right, left)[None], send_ref.shape)
    mine = jnp.where(col >= 8, right, left)
    mine = pltpu.roll(mine, jnp.bitwise_and(128 - jnp.bitwise_and(col, 7) * GROUP, 127), 1)
    for a in range(3):
        own_ref[a] = mine[3 * a : 3 * a + 3, 0:GROUP]


def totals(place, parts, node_state, w_out, copies):
    return pl.pallas_call(
        total_kernel,
        in_specs=[pl.BlockSpec(memory_space=pltpu.SMEM)] + [pl.BlockSpec(memory_space=pltpu.VMEM)] * 3,
        out_shape=[
            jax.ShapeDtypeStruct((GROUP, 64), F32),
            jax.ShapeDtypeStruct((3, 3, GROUP), F32),
            jax.ShapeDtypeStruct((16, 256), F32),
            jax.ShapeDtypeStruct((copies, 16, 128), F32),
        ],
        scratch_shapes=[pltpu.VMEM((128, 64), BF16)],
        name="totals",
    )(place, parts, node_state, w_out)


def transition_kernel(pair_ref, w_in_ref, w_out_ref, w_gate_ref, *refs):
    base_ref, gate_ref = refs[-2:]
    rows = pair_ref.shape[0]
    for i in range(0, rows, 2):
        x = pair_ref[pl.ds(i, 2)].reshape(256, 128).astype(F32)
        centred = x - jnp.mean(x, axis=1, keepdims=True)
        scale = lax.rsqrt(jnp.mean(centred * centred, axis=1, keepdims=True) + 1e-05)
        normed = (centred * scale).astype(BF16)
        hidden = jnp.maximum(dot(normed, w_in_ref[...]), 0.0).astype(BF16)
        gate = sigmoid(dot(normed, w_gate_ref[...]))
        base = x + dot(hidden, w_out_ref[...])
        base_ref[pl.ds(i, 2)] = base.astype(BF16).reshape(2, 128, 128)
        gate_ref[pl.ds(i, 2)] = gate.astype(BF16).reshape(2, 128, 128)


def transition(pair, w_in, w_out, w_gate, first, count, made=None):
    block = 16
    rows = pl.BlockSpec((block, 128, 128), lambda i: (i + first // block, 0, 0))
    whole = lambda a: pl.BlockSpec(a.shape, lambda i: (0,) * a.ndim)
    before = [] if made is None else list(made)
    shape = jax.ShapeDtypeStruct(pair.shape, BF16)
    return pl.pallas_call(
        transition_kernel,
        grid=(count // block,),
        in_specs=[rows, whole(w_in), whole(w_out), whole(w_gate)]
        + [pl.BlockSpec(memory_space=pl.ANY)] * len(before),
        out_specs=[rows, rows],
        out_shape=[shape, shape],
        input_output_aliases={4 + i: i for i in range(len(before))},
        compiler_params=pltpu.CompilerParams(vmem_limit_bytes=VMEM_LIMIT),
        cost_estimate=pl.CostEstimate(
            flops=count * 128 * 2 * 128 * 640, bytes_accessed=count * 128 * 128 * 6, transcendentals=0
        ),
        name="transition",
    )(pair, w_in, w_out, w_gate, *before)


def structure_kernel(
    place_ref,
    rows_ref,
    row_chain_ref,
    cols_ref,
    col_chain_ref,
    base_ref,
    gate_ref,
    w_in_ref,
    w_out_ref,
    out_ref,
    w_in_s,
    w_out_s,
):
    step = pl.program_id(0)

    @pl.when(step == 0)
    def _():
        w_in_s[...] = jnp.zeros_like(w_in_s)
        w_out_s[...] = jnp.zeros_like(w_out_s)
        half = (w_in_ref[...].astype(F32) * 0.5).astype(BF16)
        for k in range(2):
            w_in_s[48 * k : 48 * k + 36, 128 * k : 128 * (k + 1)] = half[0:36]
            w_in_s[48 * k + 40 : 48 * k + 46, 128 * k : 128 * (k + 1)] = half[36:42]
            w_out_s[128 * k : 128 * (k + 1), 128 * k : 128 * (k + 1)] = w_out_ref[...]

    rows = base_ref.shape[0]
    cols = cols_ref[0]
    wide = lambda v: jnp.broadcast_to(v, (8, 128))
    alpha = [wide(cols[3 + x : 4 + x, :]) for x in range(3)]
    feature = iota((8, 128), 0)
    bonds = [
        jnp.where(
            feature == 2,
            alpha[x] - wide(cols[x : x + 1, :]),
            jnp.where(feature == 3, alpha[x] - wide(cols[6 + x : 7 + x, :]), 0.0),
        )
        for x in range(3)
    ]
    chain = wide(col_chain_ref[...])
    position = iota((8, 128), 1) + place_ref[1] * 128
    centre = [(iota((8, 128), 0) + 8 * b).astype(F32) * CENTRE_STEP for b in range(5)]

    def features(row):
        p = [rows_ref[3 + x, row] for x in range(3)]
        rn = [rows_ref[x, row] - p[x] for x in range(3)]
        rc = [rows_ref[6 + x, row] - p[x] for x in range(3)]
        gap = [alpha[x] - p[x] for x in range(3)]
        square = gap[0] * gap[0] + gap[1] * gap[1] + gap[2] * gap[2]
        distance = jnp.sqrt(square)
        inverse = 1.0 / (1.0 + distance)
        vectors = [
            jnp.where(feature == 0, rn[x], jnp.where(feature == 1, rc[x], bonds[x])) for x in range(3)
        ]
        orient = (vectors[0] * gap[0] + vectors[1] * gap[1] + vectors[2] * gap[2]) * inverse
        same = jnp.where(chain == row_chain_ref[row], 1.0, 0.0)
        at = row + place_ref[0] * 256
        offset = same * (jnp.clip(position - at, -32, 32).astype(F32) * (1.0 / 32.0))
        tail = jnp.where(feature == 4, same, jnp.where(feature == 5, offset, orient))
        tail = jnp.where(feature < 6, tail, 0.0)
        basis = []
        for b in range(5):
            t = (distance - centre[b]) * 2.0
            basis.append(jnp.exp(-(t * t)))
        return basis + [tail]

    for i in range(0, rows, 2):
        row = step * rows + i
        feats = jnp.concatenate(features(row) + features(row + 1), axis=0).astype(BF16)
        half = dot_t(feats, w_in_s[...])
        hidden = (half + half * jnp.tanh(half)).astype(BF16)
        term = dot(hidden, w_out_s[...])
        for k in range(2):
            gate = gate_ref[i + k].astype(F32)
            base = base_ref[i + k].astype(F32)
            out_ref[i + k] = (base + gate * term[:, 128 * k : 128 * (k + 1)]).astype(BF16)


def structure(place, rows, row_chain, cols, col_chain, base, gate, w_in, w_out):
    block = 16
    tile = pl.BlockSpec((block, 128, 128), lambda i, place: (i, 0, 0))
    whole = lambda a: pl.BlockSpec(a.shape, lambda i, place: (0,) * a.ndim)
    return pl.pallas_call(
        structure_kernel,
        grid_spec=pltpu.PrefetchScalarGridSpec(
            num_scalar_prefetch=1,
            grid=(base.shape[0] // block,),
            in_specs=[
                pl.BlockSpec(memory_space=pltpu.SMEM),
                pl.BlockSpec(memory_space=pltpu.SMEM),
                pl.BlockSpec((1, 16, 128), lambda i, place: (place[1] // 2, 0, 0)),
                whole(col_chain),
                tile,
                tile,
                whole(w_in),
                whole(w_out),
            ],
            out_specs=tile,
            scratch_shapes=[pltpu.VMEM((96, 256), BF16), pltpu.VMEM((256, 256), BF16)],
        ),
        out_shape=jax.ShapeDtypeStruct(base.shape, BF16),
        compiler_params=pltpu.CompilerParams(vmem_limit_bytes=VMEM_LIMIT),
        name="structure",
    )(place, rows, row_chain, cols, col_chain, base, gate, w_in, w_out)


def exchange(v, axis):
    return lax.all_to_all(v, axis, split_axis=0, concat_axis=0, tiled=True)


def local(
    pair,
    node_state,
    coords,
    neighbours,
    chain,
    w_edge,
    w_radial,
    w_query,
    w_keyval,
    w_edge_kv,
    w_out,
    w_move,
    w_trans_in,
    w_trans_out,
    w_gate,
    w_feat_in,
    w_feat_out,
):
    row_devices = lax.axis_size("row")
    col_devices = lax.axis_size("col")
    row_index = lax.axis_index("row")
    col_index = lax.axis_index("col")
    place = jnp.stack([row_index, col_index]).astype(jnp.int32)
    row_chain = lax.dynamic_slice_in_dim(chain, row_index * 256, 256, 0)
    col_chain = lax.dynamic_slice_in_dim(chain, col_index * 128, 128, 0).reshape(1, 128)

    table = exchange(records(node_state, coords, row_devices * col_devices), BOTH)
    edges = select_edges(place, neighbours, pair, w_edge)
    made = transition(pair, w_trans_in, w_trans_out, w_gate, 0, 32)
    parts = edge_sums(
        place, edges, table.reshape(-1, 128), w_radial, w_query, w_keyval, w_edge_kv, w_move
    )
    held, parts = lax.optimization_barrier((made, parts))
    parts = exchange(parts, "col")
    made = transition(pair, w_trans_in, w_trans_out, w_gate, 32, 128, held)
    node_out, own, rows, send = totals(place, parts, node_state, w_out, row_devices)
    held, send = lax.optimization_barrier((made, send))
    cols = exchange(send, "row")
    base, gate = transition(pair, w_trans_in, w_trans_out, w_gate, 160, 96, held)
    pair_out = structure(place, rows, row_chain, cols, col_chain, base, gate, w_feat_in, w_feat_out)
    return (pair_out, node_out, own)


def solution(mesh):
    spread = P(None, None, BOTH)
    in_specs = (P("row", "col", None), P(BOTH, None), spread, P("row", None)) + (P(),) * 13
    out_specs = (P("row", "col", None), P(BOTH, None), spread)
    return jax.shard_map(local, mesh=mesh, in_specs=in_specs, out_specs=out_specs, check_vma=False)
```

```python
import functools

import jax
import jax.numpy as jnp
from jax import lax
from jax.experimental import pallas as pl
from jax.experimental.pallas import tpu as pltpu
from jax.sharding import PartitionSpec as P

K = 64
NRBF = 36
BOTH = ("row", "col")
F32 = jnp.float32
BF16 = jnp.bfloat16
CENTRE_STEP = 12.0 / 35.0
PIECES = 64
GROUP = 16
SLOTS = 128
GROUPS_PER_STEP = 4
VMEM_LIMIT = 48 * 1024 * 1024
SMALL_LIMIT = 8 * 1024 * 1024
BLOCK = 32
FIRST = 96
SECOND = 64


def iota(shape, dim):
    return lax.broadcasted_iota(jnp.int32, shape, dim)


def dot(a, b):
    return jnp.dot(a, b, preferred_element_type=F32)


def dot_t(a, b):
    return lax.dot_general(a, b, (((0,), (0,)), ((), ())), preferred_element_type=F32)


def dot_nt(a, b):
    return lax.dot_general(a, b, (((1,), (1,)), ((), ())), preferred_element_type=F32)


def split2(v):
    high = v.astype(BF16)
    low = (v - high.astype(F32)).astype(BF16)
    return jnp.concatenate([high, low], axis=1)


def sigmoid(v):
    return 0.5 * jnp.tanh(0.5 * v) + 0.5


def silu(v):
    half = 0.5 * v
    return half + half * jnp.tanh(half)


def record_kernel(node_ref, coords_ref, out_ref, parts_ref):
    parts_ref[...] = jnp.zeros_like(parts_ref)
    for a in range(3):
        value = coords_ref[a]
        high = value.astype(BF16).astype(F32)
        rest = value - high
        mid = rest.astype(BF16).astype(F32)
        parts_ref[pl.ds(PIECES + 3 * a, 3), :] = high
        parts_ref[pl.ds(PIECES + 16 + 3 * a, 3), :] = mid
        parts_ref[pl.ds(PIECES + 32 + 3 * a, 3), :] = rest - mid
    eye = (iota((GROUP, GROUP), 0) == iota((GROUP, GROUP), 1)).astype(F32).astype(BF16)
    widen = (iota((64, 128), 0) == iota((64, 128), 1)).astype(F32).astype(BF16)
    record = dot(node_ref[...], widen) + dot_nt(eye, parts_ref[...].astype(BF16))
    out_ref[...] = jnp.broadcast_to(record.astype(BF16)[None], out_ref.shape)


def records(node_state, coords, copies):
    return pl.pallas_call(
        record_kernel,
        out_shape=jax.ShapeDtypeStruct((copies, GROUP, 128), BF16),
        scratch_shapes=[pltpu.VMEM((128, GROUP), F32)],
        name="records",
    )(node_state, coords)


def vmem():
    return pl.BlockSpec(memory_space=pltpu.VMEM)


def in_hbm(v):
    return pltpu.with_memory_space_constraint(v, pltpu.HBM)


def hbm():
    return pl.BlockSpec(memory_space=pltpu.HBM)


def select_kernel(lists_hbm, pair_ref, found_ref, mark_ref, lists_ref, tile_ref, rank_ref, sems, lists_sem):
    groups = sems.shape[0]

    def fetch(g):
        rows = pl.ds(g * GROUP, GROUP)
        return pltpu.make_async_copy(pair_ref.at[rows], tile_ref.at[rows], sems.at[g])

    lists_copy = pltpu.make_async_copy(lists_hbm, lists_ref, lists_sem)
    lists_copy.start()
    start = lax.axis_index("col") * 128
    rows = groups * GROUP
    square = (128, 128)
    before = (iota(square, 0) < iota(square, 1)).astype(F32).astype(BF16)
    eye = (iota(square, 0) == iota(square, 1)).astype(F32).astype(BF16)
    one, other = iota((rows, rows), 0), iota((rows, rows), 1)
    earlier = (lax.shift_right_logical(one, 4) == lax.shift_right_logical(other, 4)) & (one > other)
    earlier = jnp.where(earlier, 1.0, 0.0).astype(BF16)
    lists_copy.wait()
    for g in range(groups):
        fetch(g).start()
    column = iota((128, rows), 0) + start
    chosen = jnp.zeros((128, rows), F32)
    for k in range(K):
        chosen = jnp.where(lists_ref[k : k + 1, :] == column, 1.0, chosen)
    chosen = chosen.astype(BF16)
    totals = dot_t(chosen, jnp.ones(square, BF16)).astype(BF16)
    rank = dot_t(chosen, before) + dot(earlier, totals)
    rank_ref[...] = jnp.where(dot_t(chosen, eye) > 0.0, rank, -1.0)
    slot = iota((SLOTS, 128), 0).astype(F32)

    def group(g, carry):
        fetch(g).wait()
        mark = jnp.zeros((SLOTS, 128), F32)
        picks = []
        ranks = rank_ref[pl.ds(pl.multiple_of(g * GROUP, GROUP), GROUP), :]
        for i in range(GROUP):
            hit = slot == ranks[i : i + 1, :]
            mark = jnp.where(hit, i + 1.0, mark)
            picks.append(jnp.where(hit, 1.0, 0.0).astype(BF16))
        pick = jnp.concatenate(picks, axis=1)
        spots = pl.ds(pl.multiple_of(g * SLOTS, SLOTS), SLOTS)
        tile = tile_ref[pl.ds(pl.multiple_of(g * GROUP, GROUP), GROUP)]
        found_ref[spots, :] = dot(pick, tile.reshape(GROUP * 128, 128)).astype(BF16)
        mark_ref[spots, :] = mark.astype(BF16)
        return carry

    lax.fori_loop(0, groups, group, 0, unroll=4)


def select_edges(lists, pair):
    groups = pair.shape[0] // GROUP
    return pl.pallas_call(
        select_kernel,
        in_specs=[hbm(), hbm()],
        out_specs=[vmem()] * 2,
        out_shape=[jax.ShapeDtypeStruct((groups * SLOTS, 128), BF16)] * 2,
        scratch_shapes=[
            pltpu.VMEM(lists.shape, jnp.int32),
            pltpu.VMEM(pair.shape, BF16),
            pltpu.VMEM((pair.shape[0], 128), F32),
            pltpu.SemaphoreType.DMA((groups,)),
            pltpu.SemaphoreType.DMA,
        ],
        compiler_params=pltpu.CompilerParams(vmem_limit_bytes=VMEM_LIMIT),
        cost_estimate=pl.CostEstimate(flops=3_000_000_000, bytes_accessed=9 * 2**20, transcendentals=0),
        name="select_edges",
    )(in_hbm(lists), in_hbm(pair))


def edge_kernel(
    found_ref,
    mark_ref,
    table_ref,
    w_edge_ref,
    w_radial_ref,
    w_query_ref,
    w_keyval_ref,
    w_edge_kv_ref,
    w_move_ref,
    out_ref,
    w_edge_s,
    w_keyval_s,
    w_query_s,
    w_radial_s,
    w_mix_s,
    w_move_s,
    rows_ref,
):
    col = lax.axis_index("col")
    for ref in (w_edge_s, w_keyval_s, w_query_s, w_radial_s, w_mix_s, w_move_s):
        ref[...] = jnp.zeros_like(ref)
    w_edge_s[0:64, :] = w_edge_ref[...]
    w_keyval_s[0:64, :] = w_keyval_ref[...]
    w_query_s[0:64, 0:64] = w_query_ref[...]
    w_radial_s[0:36, 0:64] = w_radial_ref[...]
    w_mix_s[0:64, :] = w_edge_kv_ref[...]
    w_move_s[0:12, 0:64] = w_move_ref[...]
    rows = table_ref[pl.ds(pl.multiple_of(lax.axis_index("row") * 256, 256), 256), :]
    rows_ref[...] = rows
    cols = table_ref[pl.ds(pl.multiple_of(col * 128, 128), 128), :]
    keyval = dot(cols, w_keyval_s[...]).astype(BF16)
    by_column = jnp.concatenate([keyval, cols], axis=1)
    lane = iota((1, 128), 1)
    source = iota((256, 256), 0)
    target = iota((256, 256), 1)
    channel = jnp.bitwise_and(source, 127)
    head = lax.shift_right_logical(channel, 4)
    for_value = (target >= 64) & (target < 128) & (lax.shift_right_logical(target - 64, 4) == head)
    for_move = (target >= 128) & (target < 140) & (jnp.bitwise_and(target, 3) == head)
    heads = jnp.where((channel < 64) & (for_value | for_move), 0.125, 0.0).astype(BF16)
    source = jnp.bitwise_and(iota((256, 128), 0), 127)
    target = iota((256, 128), 1) - PIECES
    low_atom = lax.shift_right_logical(source, 2) * 3
    spread = jnp.where(
        (source < 12) & (target >= low_atom) & (target < low_atom + 3), 1.0, 0.0
    ).astype(BF16)
    centre = lane.astype(F32) * CENTRE_STEP
    alpha = jnp.where((lane >= PIECES + 3) & (lane < PIECES + 6), 1.0, 0.0)
    per = GROUPS_PER_STEP * SLOTS
    own = GROUPS_PER_STEP * GROUP
    steps = found_ref.shape[0] // per
    shift_by = lax.shift_right_logical(iota((per, 128), 0), 7) * GROUP
    parts = []
    for step in range(steps):
        mark = mark_ref[pl.ds(step * per, per), :].astype(F32)
        residue = jnp.sum(mark, axis=1, keepdims=True) - 1.0
        pick_col = jnp.where(mark > 0.0, 1.0, 0.0).astype(BF16)
        target_row = jnp.where((lane >= shift_by) & (lane < shift_by + GROUP), lane - shift_by, -2).astype(F32)
        pick_row = jnp.where(residue == target_row, 1.0, 0.0).astype(BF16)
        rows = rows_ref[pl.ds(step * own, own), :]
        rows = jnp.concatenate([rows, jnp.zeros((128 - own, 128), BF16)], axis=0)
        from_col = dot(pick_col, by_column)
        from_row = dot(pick_row, rows)
        gap = from_col[:, 128:] - from_row
        relative = gap + pltpu.roll(gap, 112, 1) + pltpu.roll(gap, 96, 1)
        distance = jnp.sqrt(jnp.sum(relative * relative * alpha, axis=1, keepdims=True))
        offset = (distance - centre) * 2.0
        basis = jnp.exp(-(offset * offset)).astype(BF16)
        found = found_ref[pl.ds(step * per, per), :]
        hidden = silu(dot_nt(found, w_edge_s[...]) + dot(basis, w_radial_s[...])).astype(BF16)
        keyval_edge = from_col[:, :128] + dot(hidden, w_mix_s[...])
        queries = dot(from_row.astype(BF16), w_query_s[...])
        attention = 0.5 * jnp.tanh(dot(split2(queries * keyval_edge), heads)) + 0.5
        values = attention[:, :128] * keyval_edge
        moves = attention[:, 128:] * dot_nt(hidden, w_move_s[...])
        move = dot(split2(moves), spread) * relative
        both = jnp.where(lane < 64, pltpu.roll(move, 64, 1), values)
        summed = dot_t(pick_row, split2(both))
        parts.append((summed[:own, :128] + summed[:own, 128:]) * (1.0 / K))
    total = jnp.concatenate(parts, axis=0)
    atoms = rows_ref[...].astype(F32)
    atoms = atoms + pltpu.roll(atoms, 112, 1) + pltpu.roll(atoms, 96, 1)
    first = jnp.where(col == 0, 1.0, 0.0)
    total = total + jnp.where(lane < 9, pltpu.roll(atoms, 64, 1), 0.0) * first
    by_lane = jnp.transpose(total)
    groups = out_ref.shape[0]
    for d in range(groups):
        out_ref[d, 0:16, :] = total[d * GROUP : (d + 1) * GROUP, :]
        out_ref[d, 16:24, :] = by_lane[0:8, 0:128]
        out_ref[d, 24:32, :] = by_lane[0:8, 128:256]
        out_ref[d, 32:40, :] = jnp.concatenate(
            [by_lane[8:9, 0:128], by_lane[8:9, 128:256], jnp.zeros((6, 128), F32)], axis=0
        )


def edge_sums(found, mark, table, w_edge, w_radial, w_query, w_keyval, w_edge_kv, w_move):
    groups = found.shape[0] // SLOTS
    operands = (found, mark, table, w_edge, w_radial, w_query, w_keyval, w_edge_kv, w_move)
    whole = lambda shape: pl.BlockSpec(shape, lambda i: (0,) * len(shape))
    return pl.pallas_call(
        edge_kernel,
        grid=(1,),
        in_specs=[whole(a.shape) for a in operands],
        out_specs=whole((groups, 40, 128)),
        scratch_shapes=[pltpu.VMEM((128, 128), BF16)] * 6 + [pltpu.VMEM((groups * GROUP, 128), BF16)],
        out_shape=jax.ShapeDtypeStruct((groups, 40, 128), F32),
        compiler_params=pltpu.CompilerParams(vmem_limit_bytes=VMEM_LIMIT),
        cost_estimate=pl.CostEstimate(flops=2_000_000_000, bytes_accessed=3 * 2**20, transcendentals=0),
        name="edge_sums",
    )(*operands)


def total_kernel(parts_ref, node_ref, w_out_ref, node_out_ref, own_ref, rows_ref, send_ref, w_ref):
    col = lax.axis_index("col")
    total = parts_ref[0]
    for d in range(1, parts_ref.shape[0]):
        total = total + parts_ref[d]
    w_ref[...] = jnp.zeros_like(w_ref)
    w_ref[64:128, :] = w_out_ref[...]
    message = total[0:16, :].astype(BF16)
    node_out_ref[...] = node_ref[...].astype(F32) + dot(message, w_ref[...])
    left = jnp.concatenate([total[16:24, :], total[32:33, :], jnp.zeros((7, 128), F32)], axis=0)
    right = jnp.concatenate([total[24:32, :], total[33:34, :], jnp.zeros((7, 128), F32)], axis=0)
    rows_ref[:, 0:128] = left
    rows_ref[:, 128:256] = right
    odd = jnp.bitwise_and(col, 1) == 1
    send_ref[...] = jnp.broadcast_to(jnp.where(odd, right, left)[None], send_ref.shape)
    mine = jnp.where(col >= 8, right, left)
    mine = pltpu.roll(mine, jnp.bitwise_and(128 - jnp.bitwise_and(col, 7) * GROUP, 127), 1)
    for a in range(3):
        own_ref[a] = mine[3 * a : 3 * a + 3, 0:GROUP]


def totals(parts, node_state, w_out, copies):
    operands = (parts, node_state, w_out)
    shapes = ((GROUP, 64), (3, 3, GROUP), (16, 256), (copies, 16, 128))
    whole = lambda shape: pl.BlockSpec(shape, lambda i: (0,) * len(shape))
    return pl.pallas_call(
        total_kernel,
        grid=(1,),
        in_specs=[whole(a.shape) for a in operands],
        out_specs=[whole(shape) for shape in shapes],
        out_shape=[jax.ShapeDtypeStruct(shape, F32) for shape in shapes],
        scratch_shapes=[pltpu.VMEM((128, 64), BF16)],
        compiler_params=pltpu.CompilerParams(vmem_limit_bytes=SMALL_LIMIT),
        name="totals",
    )(*operands)


def transition_step(x, w_in, w_out, half_gate):
    x = x.astype(F32)
    centred = x - jnp.mean(x, axis=1, keepdims=True)
    mean = jnp.full((128, 128), 1.0 / 128.0, BF16)
    scale = lax.rsqrt(dot((centred * centred).astype(BF16), mean) + 1e-05)
    normed = (centred * scale).astype(BF16)
    hidden = jnp.maximum(dot(normed, w_in).astype(BF16), 0)
    return x + dot(hidden, w_out), jnp.tanh(dot(normed, half_gate)) + 1.0


def halved(ref):
    return (ref[...].astype(F32) * 0.5).astype(BF16)


def transition_kernel(
    first, pair_ref, w_in_ref, w_out_ref, w_gate_ref, base_ref, gate_ref, x_s, base_s, gate_s, sems, sem
):
    count = x_s.shape[0]

    def fetch(n):
        rows = pl.ds(n * BLOCK, BLOCK)
        return pltpu.make_async_copy(pair_ref.at[pl.ds(first + n * BLOCK, BLOCK)], x_s.at[rows], sems.at[n])

    for n in range(count // BLOCK):
        fetch(n).start()
    half_gate = halved(w_gate_ref)
    per = 8

    def step(n, carry):
        fetch(n).wait()
        for i in range(0, BLOCK, per):
            rows = pl.ds(n * BLOCK + i, per)
            x = x_s[rows].reshape(per * 128, 128)
            base, gate = transition_step(x, w_in_ref[...], w_out_ref[...], half_gate)
            base_s[rows] = base.astype(BF16).reshape(per, 128, 128)
            gate_s[rows] = gate.astype(BF16).reshape(per, 128, 128)
        rows = pl.ds(n * BLOCK, BLOCK)
        pltpu.make_async_copy(base_s.at[rows], base_ref.at[rows], sem).start()
        pltpu.make_async_copy(gate_s.at[rows], gate_ref.at[rows], sem).start()
        return carry

    lax.fori_loop(0, count // BLOCK, step, 0)
    pltpu.make_async_copy(base_s, base_ref, sem).wait()
    pltpu.make_async_copy(gate_s, gate_ref, sem).wait()


def transition(pair, w_in, w_out, w_gate, first, count):
    shape = (count,) + pair.shape[1:]
    return pl.pallas_call(
        functools.partial(transition_kernel, first),
        in_specs=[hbm()] + [vmem()] * 3,
        out_specs=[hbm()] * 2,
        out_shape=[pltpu.HBM(shape, BF16)] * 2,
        scratch_shapes=[pltpu.VMEM(shape, BF16)] * 3
        + [pltpu.SemaphoreType.DMA((count // BLOCK,)), pltpu.SemaphoreType.DMA],
        compiler_params=pltpu.CompilerParams(vmem_limit_bytes=VMEM_LIMIT),
        cost_estimate=pl.CostEstimate(
            flops=count * 128 * 2 * 128 * 640, bytes_accessed=count * 128 * 128 * 6, transcendentals=0
        ),
        name="transition",
    )(in_hbm(pair), w_in, w_out, w_gate)


def structure_kernel(
    counts, rows_ref, chain_ref, cols_ref, chains_ref, w_in_ref, w_out_ref, w_up_ref, w_down_ref, w_gate_ref, pair_ref, *refs
):
    held = refs[: 2 * len(counts)]
    out_ref, base_s, gate_s, made_s, w_in_s, w_out_s, sems, sem = refs[2 * len(counts) :]
    done = sum(counts)
    total = base_s.shape[0]
    blocks = total // BLOCK

    def fetch(n):
        at = n * BLOCK
        rows = pl.ds(at, BLOCK)
        if at >= done:
            return [pltpu.make_async_copy(pair_ref.at[rows], base_s.at[rows], sems.at[n])]
        part = 0
        while at >= counts[part]:
            at -= counts[part]
            part += 1
        source = pl.ds(at, BLOCK)
        return [
            pltpu.make_async_copy(held[2 * part].at[source], base_s.at[rows], sems.at[n]),
            pltpu.make_async_copy(held[2 * part + 1].at[source], gate_s.at[rows], sems.at[blocks + n]),
        ]

    for n in range(blocks):
        for copy in fetch(n):
            copy.start()
    row_index = lax.axis_index("row")
    col_index = lax.axis_index("col")
    w_in_s[...] = jnp.zeros_like(w_in_s)
    w_out_s[...] = jnp.zeros_like(w_out_s)
    half = halved(w_in_ref)
    for k in range(2):
        w_in_s[48 * k : 48 * k + 36, 128 * k : 128 * (k + 1)] = half[0:36]
        w_in_s[48 * k + 40 : 48 * k + 46, 128 * k : 128 * (k + 1)] = half[36:42]
        w_out_s[128 * k : 128 * (k + 1), 128 * k : 128 * (k + 1)] = halved(w_out_ref)
    half_gate = halved(w_gate_ref)

    cols = cols_ref[lax.shift_right_logical(col_index, 1)]
    wide = lambda v: jnp.broadcast_to(v, (8, 128))
    alpha = [wide(cols[3 + x : 4 + x, :]) for x in range(3)]
    feature = iota((8, 128), 0)
    bonds = [
        jnp.where(
            feature == 2,
            alpha[x] - wide(cols[x : x + 1, :]),
            jnp.where(feature == 3, alpha[x] - wide(cols[6 + x : 7 + x, :]), 0.0),
        )
        for x in range(3)
    ]
    chain = wide(chains_ref[pl.ds(col_index, 1), :])
    position = iota((8, 128), 1) + col_index * 128
    centre = [(iota((8, 128), 0) + 8 * b).astype(F32) * CENTRE_STEP for b in range(5)]

    def features(row):
        p = [rows_ref[3 + x, row] for x in range(3)]
        rn = [rows_ref[x, row] - p[x] for x in range(3)]
        rc = [rows_ref[6 + x, row] - p[x] for x in range(3)]
        gap = [alpha[x] - p[x] for x in range(3)]
        square = gap[0] * gap[0] + gap[1] * gap[1] + gap[2] * gap[2]
        distance = jnp.sqrt(square)
        inverse = 1.0 / (1.0 + distance)
        vectors = [
            jnp.where(feature == 0, rn[x], jnp.where(feature == 1, rc[x], bonds[x])) for x in range(3)
        ]
        orient = (vectors[0] * gap[0] + vectors[1] * gap[1] + vectors[2] * gap[2]) * inverse
        at = row + row_index * 256
        same = jnp.where(chain == chain_ref[at], 1.0, 0.0)
        offset = same * (jnp.clip(position - at, -32, 32).astype(F32) * (1.0 / 32.0))
        tail = jnp.where(feature == 4, same, jnp.where(feature == 5, offset, orient))
        tail = jnp.where(feature < 6, tail, 0.0)
        basis = []
        for b in range(5):
            t = (distance - centre[b]) * 2.0
            basis.append(jnp.exp(-(t * t)))
        return basis + [tail]

    per = 16

    def terms(start):
        feats = []
        for u in range(per // 2):
            row = start + 2 * u
            feats.append(jnp.concatenate(features(row) + features(row + 1), axis=0).astype(BF16))
        half = dot_t(jnp.concatenate(feats, axis=1), w_in_s[...])
        hidden = (half + half * jnp.tanh(half)).astype(BF16)
        term = dot(hidden, w_out_s[...])
        return [
            term[128 * (u // 2) : 128 * (u // 2 + 1), 128 * (u % 2) : 128 * (u % 2 + 1)] for u in range(per)
        ]

    def finish_held(start):
        for u, term in enumerate(terms(start)):
            gate = gate_s[start + u].astype(F32)
            made_s[start + u] = (base_s[start + u].astype(F32) + gate * term).astype(BF16)

    def finish_whole(start):
        term = terms(start)
        for i in range(0, per, 8):
            x = base_s[pl.ds(start + i, 8)].reshape(8 * 128, 128)
            base, gate = transition_step(x, w_up_ref[...], w_down_ref[...], half_gate)
            for u in range(8):
                spot = slice(128 * u, 128 * (u + 1))
                made_s[start + i + u] = (base[spot] + gate[spot] * term[i + u]).astype(BF16)

    def send(n):
        rows = pl.ds(n * BLOCK, BLOCK)
        pltpu.make_async_copy(made_s.at[rows], out_ref.at[rows], sem).start()

    def await_block(n, pair_too):
        rows = pl.ds(n * BLOCK, BLOCK)
        pltpu.make_async_copy(pair_ref.at[rows], base_s.at[rows], sems.at[n]).wait()
        if pair_too:
            pltpu.make_async_copy(pair_ref.at[rows], gate_s.at[rows], sems.at[blocks + n]).wait()

    def step(finish, pair_too, n, carry):
        await_block(n, pair_too)
        for i in range(0, BLOCK, per):
            finish(n * BLOCK + i)
        send(n)
        return carry

    lax.fori_loop(0, done // BLOCK, functools.partial(step, finish_held, True), 0)
    lax.fori_loop(done // BLOCK, blocks, functools.partial(step, finish_whole, False), 0)
    pltpu.make_async_copy(made_s, out_ref, sem).wait()


def structure(rows, chain, cols, w_in, w_out, w_up, w_down, w_gate, pair, held):
    smem = pl.BlockSpec(memory_space=pltpu.SMEM)
    counts = tuple(base.shape[0] for base in held[0::2])
    blocks = pair.shape[0] // BLOCK
    return pl.pallas_call(
        functools.partial(structure_kernel, counts),
        in_specs=[smem, smem] + [vmem()] * 7 + [hbm()] * (1 + len(held)),
        out_specs=hbm(),
        scratch_shapes=[pltpu.VMEM(pair.shape, BF16)] * 3
        + [
            pltpu.VMEM((96, 256), BF16),
            pltpu.VMEM((256, 256), BF16),
            pltpu.SemaphoreType.DMA((2 * blocks,)),
            pltpu.SemaphoreType.DMA,
        ],
        out_shape=jax.ShapeDtypeStruct(pair.shape, BF16),
        compiler_params=pltpu.CompilerParams(vmem_limit_bytes=VMEM_LIMIT),
        name="structure",
    )(rows, chain, cols, chain.reshape(-1, 128), w_in, w_out, w_up, w_down, w_gate, in_hbm(pair), *map(in_hbm, held))


def exchange(v, axis):
    return lax.all_to_all(v, axis, split_axis=0, concat_axis=0, tiled=True)


def local(
    pair,
    node_state,
    coords,
    neighbours,
    chain,
    w_edge,
    w_radial,
    w_query,
    w_keyval,
    w_edge_kv,
    w_out,
    w_move,
    w_trans_in,
    w_trans_out,
    w_gate,
    w_feat_in,
    w_feat_out,
):
    row_devices = lax.axis_size("row")
    col_devices = lax.axis_size("col")
    step = functools.partial(transition, w_in=w_trans_in, w_out=w_trans_out, w_gate=w_gate)

    table = exchange(records(node_state, coords, row_devices * col_devices), BOTH)
    found, mark = select_edges(neighbours.T, pair)
    parts = edge_sums(
        found,
        mark,
        table.reshape(-1, 128),
        w_edge.T,
        w_radial,
        w_query,
        w_keyval,
        w_edge_kv,
        w_move.T,
    )
    pair, parts = lax.optimization_barrier((pair, parts))
    parts = exchange(parts, "col")
    held = step(pair, first=0, count=FIRST)
    node_out, own, rows, send = totals(parts, node_state, w_out, row_devices)
    pair, send = lax.optimization_barrier((pair, send))
    cols = exchange(send, "row")
    held += step(pair, first=FIRST, count=SECOND)
    pair_out = structure(
        rows, chain, cols, w_feat_in, w_feat_out, w_trans_in, w_trans_out, w_gate, pair, held
    )
    return (pair_out, node_out, own)


def solution(mesh):
    spread = P(None, None, BOTH)
    in_specs = (P("row", "col", None), P(BOTH, None), spread, P("row", None)) + (P(),) * 13
    out_specs = (P("row", "col", None), P(BOTH, None), spread)
    return jax.shard_map(local, mesh=mesh, in_specs=in_specs, out_specs=out_specs, check_vma=False)
```

```python
import functools

import jax
import jax.numpy as jnp
from jax import lax
from jax.experimental import pallas as pl
from jax.experimental.pallas import tpu as pltpu
from jax.sharding import PartitionSpec as P

K = 64
NRBF = 36
BOTH = ("row", "col")
F32 = jnp.float32
BF16 = jnp.bfloat16
CENTRE_STEP = 12.0 / 35.0
PIECES = 64
GROUP = 16
SLOTS = 128
GROUPS_PER_STEP = 8
VMEM_LIMIT = 48 * 1024 * 1024
SMALL_LIMIT = 8 * 1024 * 1024
BLOCK = 32
STEP = 8
HELD_STEP = 16
PARTS = (0, 96, 32)


def iota(shape, dim):
    return lax.broadcasted_iota(jnp.int32, shape, dim)


def dot(a, b):
    return jnp.dot(a, b, preferred_element_type=F32)


def dot_t(a, b):
    return lax.dot_general(a, b, (((0,), (0,)), ((), ())), preferred_element_type=F32)


def dot_nt(a, b):
    return lax.dot_general(a, b, (((1,), (1,)), ((), ())), preferred_element_type=F32)


def split2(v):
    high = v.astype(BF16)
    low = (v - high.astype(F32)).astype(BF16)
    return jnp.concatenate([high, low], axis=1)


def sigmoid(v):
    return 0.5 * jnp.tanh(0.5 * v) + 0.5


def silu(v):
    half = 0.5 * v
    return half + half * jnp.tanh(half)


def record_kernel(node_ref, coords_ref, out_ref, parts_ref):
    parts_ref[...] = jnp.zeros_like(parts_ref)
    for a in range(3):
        value = coords_ref[a]
        high = value.astype(BF16).astype(F32)
        rest = value - high
        mid = rest.astype(BF16).astype(F32)
        parts_ref[pl.ds(PIECES + 3 * a, 3), :] = high
        parts_ref[pl.ds(PIECES + 16 + 3 * a, 3), :] = mid
        parts_ref[pl.ds(PIECES + 32 + 3 * a, 3), :] = rest - mid
    eye = (iota((GROUP, GROUP), 0) == iota((GROUP, GROUP), 1)).astype(F32).astype(BF16)
    widen = (iota((64, 128), 0) == iota((64, 128), 1)).astype(F32).astype(BF16)
    record = dot(node_ref[...], widen) + dot_nt(eye, parts_ref[...].astype(BF16))
    out_ref[...] = jnp.broadcast_to(record.astype(BF16)[None], out_ref.shape)


def records(node_state, coords, copies):
    return pl.pallas_call(
        record_kernel,
        out_shape=jax.ShapeDtypeStruct((copies, GROUP, 128), BF16),
        scratch_shapes=[pltpu.VMEM((128, GROUP), F32)],
        name="records",
    )(node_state, coords)


def vmem():
    return pl.BlockSpec(memory_space=pltpu.VMEM)


def in_hbm(v):
    return pltpu.with_memory_space_constraint(v, pltpu.HBM)


def hbm():
    return pl.BlockSpec(memory_space=pltpu.HBM)


def select_kernel(
    lists_hbm,
    pair_ref,
    w_edge_hbm,
    edge_ref,
    pick_col_ref,
    pick_row_ref,
    lists_ref,
    tile_ref,
    rank_ref,
    w_edge_ref,
    w_edge_s,
    sems,
    lists_sem,
    w_edge_sem,
):
    groups = sems.shape[0]

    def fetch(g):
        rows = pl.ds(g * GROUP, GROUP)
        return pltpu.make_async_copy(pair_ref.at[rows], tile_ref.at[rows], sems.at[g])

    lists_copy = pltpu.make_async_copy(lists_hbm, lists_ref, lists_sem)
    lists_copy.start()
    w_edge_copy = pltpu.make_async_copy(w_edge_hbm, w_edge_ref, w_edge_sem)
    w_edge_copy.start()
    start = lax.axis_index("col") * 128
    rows = groups * GROUP
    square = (128, 128)
    before = (iota(square, 0) < iota(square, 1)).astype(F32).astype(BF16)
    eye = (iota(square, 0) == iota(square, 1)).astype(F32).astype(BF16)
    one, other = iota((rows, rows), 0), iota((rows, rows), 1)
    earlier = (lax.shift_right_logical(one, 4) == lax.shift_right_logical(other, 4)) & (one > other)
    earlier = jnp.where(earlier, 1.0, 0.0).astype(BF16)
    lists_copy.wait()
    for g in range(groups):
        fetch(g).start()
    column = iota((128, rows), 0) + start
    chosen = jnp.zeros((128, rows), F32)
    for k in range(K):
        chosen = jnp.where(lists_ref[k : k + 1, :] == column, 1.0, chosen)
    chosen = chosen.astype(BF16)
    totals = dot_t(chosen, jnp.ones(square, BF16)).astype(BF16)
    rank = dot_t(chosen, before) + dot(earlier, totals)
    rank_ref[...] = jnp.where(dot_t(chosen, eye) > 0.0, rank, -1.0)
    slot = iota((SLOTS, 128), 0).astype(F32)
    lane = iota((1, 128), 1)
    w_edge_copy.wait()
    w_edge_s[...] = jnp.zeros_like(w_edge_s)
    w_edge_s[0:64, :] = w_edge_ref[...]

    def group(g, carry):
        fetch(g).wait()
        mark = jnp.zeros((SLOTS, 128), F32)
        picks = []
        ranks = rank_ref[pl.ds(pl.multiple_of(g * GROUP, GROUP), GROUP), :]
        for i in range(GROUP):
            hit = slot == ranks[i : i + 1, :]
            mark = jnp.where(hit, i + 1.0, mark)
            picks.append(jnp.where(hit, 1.0, 0.0).astype(BF16))
        pick = jnp.concatenate(picks, axis=1)
        spots = pl.ds(pl.multiple_of(g * SLOTS, SLOTS), SLOTS)
        tile = tile_ref[pl.ds(pl.multiple_of(g * GROUP, GROUP), GROUP)]
        found = dot(pick, tile.reshape(GROUP * 128, 128)).astype(BF16)
        edge_ref[spots, :] = dot_nt(found, w_edge_s[...])
        pick_col_ref[spots, :] = jnp.where(mark > 0.0, 1.0, 0.0).astype(BF16)
        own = lane - lax.rem(g, GROUPS_PER_STEP) * GROUP
        own = jnp.where((own >= 0) & (own < GROUP), own + 1, -1).astype(F32)
        residue = jnp.sum(mark, axis=1, keepdims=True)
        pick_row_ref[spots, :] = jnp.where(residue == own, 1.0, 0.0).astype(BF16)
        return carry

    lax.fori_loop(0, groups, group, 0, unroll=4)


def select_edges(lists, pair, w_edge):
    groups = pair.shape[0] // GROUP
    shape = (groups * SLOTS, 128)
    return pl.pallas_call(
        select_kernel,
        in_specs=[hbm(), hbm(), hbm()],
        out_specs=[vmem()] * 3,
        out_shape=[jax.ShapeDtypeStruct(shape, dtype) for dtype in (F32, BF16, BF16)],
        scratch_shapes=[
            pltpu.VMEM(lists.shape, jnp.int32),
            pltpu.VMEM(pair.shape, BF16),
            pltpu.VMEM((pair.shape[0], 128), F32),
            pltpu.VMEM(w_edge.shape, BF16),
            pltpu.VMEM((128, 128), BF16),
            pltpu.SemaphoreType.DMA((groups,)),
            pltpu.SemaphoreType.DMA,
            pltpu.SemaphoreType.DMA,
        ],
        compiler_params=pltpu.CompilerParams(vmem_limit_bytes=VMEM_LIMIT),
        cost_estimate=pl.CostEstimate(flops=3_000_000_000, bytes_accessed=9 * 2**20, transcendentals=0),
        name="select_edges",
    )(in_hbm(lists), in_hbm(pair), in_hbm(w_edge))


def edge_kernel(
    edge_ref,
    pick_col_ref,
    pick_row_ref,
    table_ref,
    w_radial_ref,
    w_query_ref,
    w_keyval_ref,
    w_edge_kv_ref,
    w_move_ref,
    out_ref,
    w_keyval_s,
    w_query_s,
    w_radial_s,
    w_mix_s,
    w_move_s,
    rows_ref,
):
    col = lax.axis_index("col")
    for ref in (w_keyval_s, w_query_s, w_radial_s, w_mix_s, w_move_s):
        ref[...] = jnp.zeros_like(ref)
    w_keyval_s[0:64, :] = w_keyval_ref[...]
    w_query_s[0:64, 0:64] = w_query_ref[...]
    w_radial_s[0:36, 0:64] = w_radial_ref[...]
    w_mix_s[0:64, :] = w_edge_kv_ref[...]
    w_move_s[0:12, 0:64] = w_move_ref[...]
    rows = table_ref[pl.ds(pl.multiple_of(lax.axis_index("row") * 256, 256), 256), :]
    rows_ref[...] = rows
    cols = table_ref[pl.ds(pl.multiple_of(col * 128, 128), 128), :]
    keyval = dot(cols, w_keyval_s[...]).astype(BF16)
    by_column = jnp.concatenate([keyval, cols], axis=1)
    lane = iota((1, 128), 1)
    source = iota((256, 256), 0)
    target = iota((256, 256), 1)
    channel = jnp.bitwise_and(source, 127)
    head = lax.shift_right_logical(channel, 4)
    for_value = (target >= 64) & (target < 128) & (lax.shift_right_logical(target - 64, 4) == head)
    for_move = (target >= 128) & (target < 140) & (jnp.bitwise_and(target, 3) == head)
    heads = jnp.where((channel < 64) & (for_value | for_move), 0.125, 0.0).astype(BF16)
    source = jnp.bitwise_and(iota((256, 128), 0), 127)
    target = iota((256, 128), 1) - PIECES
    low_atom = lax.shift_right_logical(source, 2) * 3
    spread = jnp.where(
        (source < 12) & (target >= low_atom) & (target < low_atom + 3), 1.0, 0.0
    ).astype(BF16)
    centre = lane.astype(F32) * CENTRE_STEP
    alpha = jnp.where((lane >= PIECES + 3) & (lane < PIECES + 6), 1.0, 0.0)
    per = GROUPS_PER_STEP * SLOTS
    own = GROUPS_PER_STEP * GROUP
    steps = edge_ref.shape[0] // per
    parts = []
    for step in range(steps):
        spots = pl.ds(step * per, per)
        pick_col = pick_col_ref[spots, :]
        pick_row = pick_row_ref[spots, :]
        rows = rows_ref[pl.ds(step * own, own), :]
        from_col = dot(pick_col, by_column)
        from_row = dot(pick_row, rows)
        gap = from_col[:, 128:] - from_row
        relative = gap + pltpu.roll(gap, 112, 1) + pltpu.roll(gap, 96, 1)
        distance = jnp.sqrt(jnp.sum(relative * relative * alpha, axis=1, keepdims=True))
        offset = (distance - centre) * 2.0
        basis = jnp.exp(-(offset * offset)).astype(BF16)
        hidden = silu(edge_ref[spots, :] + dot(basis, w_radial_s[...])).astype(BF16)
        keyval_edge = from_col[:, :128] + dot(hidden, w_mix_s[...])
        queries = dot(from_row.astype(BF16), w_query_s[...])
        attention = 0.5 * jnp.tanh(dot(split2(queries * keyval_edge), heads)) + 0.5
        values = attention[:, :128] * keyval_edge
        moves = attention[:, 128:] * dot_nt(hidden, w_move_s[...])
        move = dot(split2(moves), spread) * relative
        both = jnp.where(lane < 64, pltpu.roll(move, 64, 1), values)
        summed = dot_t(pick_row, split2(both))
        parts.append((summed[:own, :128] + summed[:own, 128:]) * (1.0 / K))
    total = jnp.concatenate(parts, axis=0)
    atoms = rows_ref[...].astype(F32)
    atoms = atoms + pltpu.roll(atoms, 112, 1) + pltpu.roll(atoms, 96, 1)
    first = jnp.where(col == 0, 1.0, 0.0)
    total = total + jnp.where(lane < 9, pltpu.roll(atoms, 64, 1), 0.0) * first
    by_lane = jnp.transpose(total)
    groups = out_ref.shape[0]
    for d in range(groups):
        out_ref[d, 0:16, :] = total[d * GROUP : (d + 1) * GROUP, :]
        out_ref[d, 16:24, :] = by_lane[0:8, 0:128]
        out_ref[d, 24:32, :] = by_lane[0:8, 128:256]
        out_ref[d, 32:40, :] = jnp.concatenate(
            [by_lane[8:9, 0:128], by_lane[8:9, 128:256], jnp.zeros((6, 128), F32)], axis=0
        )


def edge_sums(edge, pick_col, pick_row, table, w_radial, w_query, w_keyval, w_edge_kv, w_move):
    groups = edge.shape[0] // SLOTS
    operands = (edge, pick_col, pick_row, table, w_radial, w_query, w_keyval, w_edge_kv, w_move)
    whole = lambda shape: pl.BlockSpec(shape, lambda i: (0,) * len(shape))
    return pl.pallas_call(
        edge_kernel,
        grid=(1,),
        in_specs=[vmem()] * 4 + [whole(a.shape) for a in operands[4:]],
        out_specs=whole((groups, 40, 128)),
        scratch_shapes=[pltpu.VMEM((128, 128), BF16)] * 5 + [pltpu.VMEM((groups * GROUP, 128), BF16)],
        out_shape=jax.ShapeDtypeStruct((groups, 40, 128), F32),
        compiler_params=pltpu.CompilerParams(vmem_limit_bytes=VMEM_LIMIT),
        cost_estimate=pl.CostEstimate(flops=2_000_000_000, bytes_accessed=3 * 2**20, transcendentals=0),
        name="edge_sums",
    )(*operands)


def total_kernel(parts_ref, node_ref, w_out_ref, node_out_ref, own_ref, rows_ref, send_ref, w_ref):
    col = lax.axis_index("col")
    total = parts_ref[0]
    for d in range(1, parts_ref.shape[0]):
        total = total + parts_ref[d]
    w_ref[...] = jnp.zeros_like(w_ref)
    w_ref[64:128, :] = w_out_ref[...]
    message = total[0:16, :].astype(BF16)
    node_out_ref[...] = node_ref[...].astype(F32) + dot(message, w_ref[...])
    left = jnp.concatenate([total[16:24, :], total[32:33, :], jnp.zeros((7, 128), F32)], axis=0)
    right = jnp.concatenate([total[24:32, :], total[33:34, :], jnp.zeros((7, 128), F32)], axis=0)
    rows_ref[:, 0:128] = left
    rows_ref[:, 128:256] = right
    odd = jnp.bitwise_and(col, 1) == 1
    send_ref[...] = jnp.broadcast_to(jnp.where(odd, right, left)[None], send_ref.shape)
    mine = jnp.where(col >= 8, right, left)
    mine = pltpu.roll(mine, jnp.bitwise_and(128 - jnp.bitwise_and(col, 7) * GROUP, 127), 1)
    for a in range(3):
        own_ref[a] = mine[3 * a : 3 * a + 3, 0:GROUP]


def totals(parts, node_state, w_out, copies):
    operands = (parts, node_state, w_out)
    shapes = ((GROUP, 64), (3, 3, GROUP), (16, 256), (copies, 16, 128))
    whole = lambda shape: pl.BlockSpec(shape, lambda i: (0,) * len(shape))
    return pl.pallas_call(
        total_kernel,
        grid=(1,),
        in_specs=[whole(a.shape) for a in operands],
        out_specs=[whole(shape) for shape in shapes],
        out_shape=[jax.ShapeDtypeStruct(shape, F32) for shape in shapes],
        scratch_shapes=[pltpu.VMEM((128, 64), BF16)],
        compiler_params=pltpu.CompilerParams(vmem_limit_bytes=SMALL_LIMIT),
        name="totals",
    )(*operands)


def transition_step(x, w_in, w_out, half_gate):
    x = x.astype(F32)
    centred = x - jnp.mean(x, axis=1, keepdims=True)
    mean = jnp.full((128, 128), 1.0 / 128.0, BF16)
    scale = lax.rsqrt(dot((centred * centred).astype(BF16), mean) + 1e-05)
    normed = (centred * scale).astype(BF16)
    hidden = jnp.maximum(dot(normed, w_in).astype(BF16), 0)
    return x + dot(hidden, w_out), jnp.tanh(dot(normed, half_gate)) + 1.0


def halved(ref):
    return (ref[...].astype(F32) * 0.5).astype(BF16)


def transition_kernel(first, pair_ref, w_in_ref, w_out_ref, w_gate_ref, base_ref, gate_ref, x_s, *refs):
    base_s, gate_s = refs[:2] if len(refs) == 4 else (base_ref, gate_ref)
    sems, sem = refs[-2:]
    count = x_s.shape[0]

    def fetch(n):
        rows = pl.ds(n * BLOCK, BLOCK)
        return pltpu.make_async_copy(pair_ref.at[pl.ds(first + n * BLOCK, BLOCK)], x_s.at[rows], sems.at[n])

    for n in range(count // BLOCK):
        fetch(n).start()
    half_gate = halved(w_gate_ref)

    def step(n, carry):
        fetch(n).wait()
        for i in range(0, BLOCK, STEP):
            rows = pl.ds(n * BLOCK + i, STEP)
            x = x_s[rows].reshape(STEP * 128, 128)
            base, gate = transition_step(x, w_in_ref[...], w_out_ref[...], half_gate)
            base_s[rows] = base.astype(BF16).reshape(STEP, 128, 128)
            gate_s[rows] = gate.astype(BF16).reshape(STEP, 128, 128)
        if base_s is not base_ref:
            rows = pl.ds(n * BLOCK, BLOCK)
            pltpu.make_async_copy(base_s.at[rows], base_ref.at[rows], sem).start()
            pltpu.make_async_copy(gate_s.at[rows], gate_ref.at[rows], sem).start()
        return carry

    lax.fori_loop(0, count // BLOCK, step, 0)
    if base_s is not base_ref:
        pltpu.make_async_copy(base_s, base_ref, sem).wait()
        pltpu.make_async_copy(gate_s, gate_ref, sem).wait()


def transition(pair, w_in, w_out, w_gate, first, count, keep=False):
    shape = (count,) + pair.shape[1:]
    return pl.pallas_call(
        functools.partial(transition_kernel, first),
        in_specs=[hbm()] + [vmem()] * 3,
        out_specs=[vmem() if keep else hbm()] * 2,
        out_shape=[(pltpu.VMEM if keep else pltpu.HBM)(shape, BF16)] * 2,
        scratch_shapes=[pltpu.VMEM(shape, BF16)] * (1 if keep else 3)
        + [pltpu.SemaphoreType.DMA((count // BLOCK,)), pltpu.SemaphoreType.DMA],
        compiler_params=pltpu.CompilerParams(vmem_limit_bytes=VMEM_LIMIT),
        cost_estimate=pl.CostEstimate(
            flops=count * 128 * 2 * 128 * 640, bytes_accessed=count * 128 * 128 * 6, transcendentals=0
        ),
        name="transition",
    )(in_hbm(pair), w_in, w_out, w_gate)


def structure_kernel(
    counts, rows_ref, chain_ref, cols_ref, chains_ref, w_in_ref, w_out_ref, w_up_ref, w_down_ref, w_gate_ref, pair_ref, *refs
):
    held = refs[: 2 * len(counts)]
    out_ref, base_s, gate_s, made_s, w_in_s, w_out_s, sems, sem = refs[2 * len(counts) :]
    done = sum(counts)
    total = base_s.shape[0]
    blocks = total // BLOCK

    def fetch(n):
        at = n * BLOCK
        rows = pl.ds(at, BLOCK)
        if at >= done:
            return [pltpu.make_async_copy(pair_ref.at[rows], base_s.at[rows], sems.at[n])]
        part = 0
        while at >= counts[part]:
            at -= counts[part]
            part += 1
        if part == len(counts) - 1:
            return []
        source = pl.ds(at, BLOCK)
        return [
            pltpu.make_async_copy(held[2 * part].at[source], base_s.at[rows], sems.at[n]),
            pltpu.make_async_copy(held[2 * part + 1].at[source], gate_s.at[rows], sems.at[blocks + n]),
        ]

    for n in range(blocks):
        for copy in fetch(n):
            copy.start()
    row_index = lax.axis_index("row")
    col_index = lax.axis_index("col")
    w_in_s[...] = jnp.zeros_like(w_in_s)
    w_out_s[...] = jnp.zeros_like(w_out_s)
    half = halved(w_in_ref)
    for k in range(2):
        w_in_s[48 * k : 48 * k + 36, 128 * k : 128 * (k + 1)] = half[0:36]
        w_in_s[48 * k + 40 : 48 * k + 46, 128 * k : 128 * (k + 1)] = half[36:42]
        w_out_s[128 * k : 128 * (k + 1), 128 * k : 128 * (k + 1)] = halved(w_out_ref)
    half_gate = halved(w_gate_ref)

    cols = cols_ref[lax.shift_right_logical(col_index, 1)]
    wide = lambda v: jnp.broadcast_to(v, (8, 128))
    alpha = [wide(cols[3 + x : 4 + x, :]) for x in range(3)]
    feature = iota((8, 128), 0)
    bonds = [
        jnp.where(
            feature == 2,
            alpha[x] - wide(cols[x : x + 1, :]),
            jnp.where(feature == 3, alpha[x] - wide(cols[6 + x : 7 + x, :]), 0.0),
        )
        for x in range(3)
    ]
    chain = wide(chains_ref[pl.ds(col_index, 1), :])
    position = iota((8, 128), 1) + col_index * 128
    centre = [(iota((8, 128), 0) + 8 * b).astype(F32) * CENTRE_STEP for b in range(5)]

    def features(row):
        p = [rows_ref[3 + x, row] for x in range(3)]
        rn = [rows_ref[x, row] - p[x] for x in range(3)]
        rc = [rows_ref[6 + x, row] - p[x] for x in range(3)]
        gap = [alpha[x] - p[x] for x in range(3)]
        square = gap[0] * gap[0] + gap[1] * gap[1] + gap[2] * gap[2]
        distance = jnp.sqrt(square)
        inverse = 1.0 / (1.0 + distance)
        vectors = [
            jnp.where(feature == 0, rn[x], jnp.where(feature == 1, rc[x], bonds[x])) for x in range(3)
        ]
        orient = (vectors[0] * gap[0] + vectors[1] * gap[1] + vectors[2] * gap[2]) * inverse
        at = row + row_index * 256
        same = jnp.where(chain == chain_ref[at], 1.0, 0.0)
        offset = same * (jnp.clip(position - at, -32, 32).astype(F32) * (1.0 / 32.0))
        tail = jnp.where(feature == 4, same, jnp.where(feature == 5, offset, orient))
        tail = jnp.where(feature < 6, tail, 0.0)
        basis = []
        for b in range(5):
            t = (distance - centre[b]) * 2.0
            basis.append(jnp.exp(-(t * t)))
        return basis + [tail]

    def terms(start, per):
        feats = []
        for u in range(per // 2):
            row = start + 2 * u
            feats.append(jnp.concatenate(features(row) + features(row + 1), axis=0).astype(BF16))
        half = dot_t(jnp.concatenate(feats, axis=1), w_in_s[...])
        hidden = (half + half * jnp.tanh(half)).astype(BF16)
        term = dot(hidden, w_out_s[...])
        return [
            term[128 * (u // 2) : 128 * (u // 2 + 1), 128 * (u % 2) : 128 * (u % 2 + 1)] for u in range(per)
        ]

    def finish_held(start, base_ref=base_s, gate_ref=gate_s, first=0):
        for u, term in enumerate(terms(start, HELD_STEP)):
            gate = gate_ref[start - first + u].astype(F32)
            made_s[start + u] = (base_ref[start - first + u].astype(F32) + gate * term).astype(BF16)

    def finish_whole(start):
        term = terms(start, STEP)
        x = base_s[pl.ds(start, STEP)].reshape(STEP * 128, 128)
        base, gate = transition_step(x, w_up_ref[...], w_down_ref[...], half_gate)
        for u in range(STEP):
            spot = slice(128 * u, 128 * (u + 1))
            made_s[start + u] = (base[spot] + gate[spot] * term[u]).astype(BF16)

    def send(n):
        rows = pl.ds(n * BLOCK, BLOCK)
        pltpu.make_async_copy(made_s.at[rows], out_ref.at[rows], sem).start()

    def await_block(n, pair_too):
        rows = pl.ds(n * BLOCK, BLOCK)
        pltpu.make_async_copy(pair_ref.at[rows], base_s.at[rows], sems.at[n]).wait()
        if pair_too:
            pltpu.make_async_copy(pair_ref.at[rows], gate_s.at[rows], sems.at[blocks + n]).wait()

    def step(finish, copies, per, n, carry):
        if copies:
            await_block(n, copies == 2)
        for i in range(0, BLOCK, per):
            finish(n * BLOCK + i)
        send(n)
        return carry

    copied = done - counts[-1]
    finish_kept = functools.partial(
        finish_held, base_ref=held[-2], gate_ref=held[-1], first=copied
    )
    kept_step = functools.partial(step, finish_kept, 0, HELD_STEP)
    lax.fori_loop(copied // BLOCK, done // BLOCK, kept_step, 0)
    lax.fori_loop(0, copied // BLOCK, functools.partial(step, finish_held, 2, HELD_STEP), 0)
    lax.fori_loop(done // BLOCK, blocks, functools.partial(step, finish_whole, 1, STEP), 0)
    pltpu.make_async_copy(made_s, out_ref, sem).wait()


def structure(rows, chain, cols, w_in, w_out, w_up, w_down, w_gate, pair, held):
    smem = pl.BlockSpec(memory_space=pltpu.SMEM)
    counts = tuple(base.shape[0] for base in held[0::2])
    blocks = pair.shape[0] // BLOCK
    return pl.pallas_call(
        functools.partial(structure_kernel, counts),
        in_specs=[smem, smem] + [vmem()] * 7 + [hbm()] * (len(held) - 1) + [vmem()] * 2,
        out_specs=hbm(),
        scratch_shapes=[pltpu.VMEM(pair.shape, BF16)] * 3
        + [
            pltpu.VMEM((96, 256), BF16),
            pltpu.VMEM((256, 256), BF16),
            pltpu.SemaphoreType.DMA((2 * blocks,)),
            pltpu.SemaphoreType.DMA,
        ],
        out_shape=jax.ShapeDtypeStruct(pair.shape, BF16),
        compiler_params=pltpu.CompilerParams(vmem_limit_bytes=VMEM_LIMIT),
        name="structure",
    )(rows, chain, cols, chain.reshape(-1, 128), w_in, w_out, w_up, w_down, w_gate, in_hbm(pair), *map(in_hbm, held[:-2]), *held[-2:])


def exchange(v, axis):
    return lax.all_to_all(v, axis, split_axis=0, concat_axis=0, tiled=True)


def local(
    pair,
    node_state,
    coords,
    neighbours,
    chain,
    w_edge,
    w_radial,
    w_query,
    w_keyval,
    w_edge_kv,
    w_out,
    w_move,
    w_trans_in,
    w_trans_out,
    w_gate,
    w_feat_in,
    w_feat_out,
):
    row_devices = lax.axis_size("row")
    col_devices = lax.axis_size("col")
    step = functools.partial(transition, w_in=w_trans_in, w_out=w_trans_out, w_gate=w_gate)

    table = exchange(records(node_state, coords, row_devices * col_devices), BOTH)
    edge, pick_col, pick_row = select_edges(neighbours.T, pair, w_edge.T)
    pair, edge = lax.optimization_barrier((pair, edge))
    held = step(pair, first=0, count=PARTS[0]) if PARTS[0] else []
    parts = edge_sums(
        edge,
        pick_col,
        pick_row,
        table.reshape(-1, 128),
        w_radial,
        w_query,
        w_keyval,
        w_edge_kv,
        w_move.T,
    )
    pair, parts, held = lax.optimization_barrier((pair, parts, held))
    parts = exchange(parts, "col")
    held += step(pair, first=PARTS[0], count=PARTS[1])
    node_out, own, rows, send = totals(parts, node_state, w_out, row_devices)
    pair, send, held = lax.optimization_barrier((pair, send, held))
    cols = exchange(send, "row")
    held += step(pair, first=PARTS[0] + PARTS[1], count=PARTS[2], keep=True)
    pair_out = structure(
        rows, chain, cols, w_feat_in, w_feat_out, w_trans_in, w_trans_out, w_gate, pair, held
    )
    return (pair_out, node_out, own)


def solution(mesh):
    spread = P(None, None, BOTH)
    in_specs = (P("row", "col", None), P(BOTH, None), spread, P("row", None)) + (P(),) * 13
    out_specs = (P("row", "col", None), P(BOTH, None), spread)
    return jax.shard_map(local, mesh=mesh, in_specs=in_specs, out_specs=out_specs, check_vma=False)
```

```python
import functools

import jax
import jax.numpy as jnp
from jax import lax
from jax.experimental import pallas as pl
from jax.experimental.pallas import tpu as pltpu
from jax.sharding import PartitionSpec as P

K = 64
NRBF = 36
BOTH = ("row", "col")
F32 = jnp.float32
BF16 = jnp.bfloat16
CENTRE_STEP = 12.0 / 35.0
PIECES = 64
GROUP = 16
SLOTS = 128
GROUPS_PER_STEP = 8
VMEM_LIMIT = 48 * 1024 * 1024
SMALL_LIMIT = 8 * 1024 * 1024
BLOCK = 32
STEP = 8
HELD_STEP = 16
PARTS = (0, 96, 32)


def iota(shape, dim):
    return lax.broadcasted_iota(jnp.int32, shape, dim)


def dot(a, b):
    return jnp.dot(a, b, preferred_element_type=F32)


def dot_t(a, b):
    return lax.dot_general(a, b, (((0,), (0,)), ((), ())), preferred_element_type=F32)


def dot_nt(a, b):
    return lax.dot_general(a, b, (((1,), (1,)), ((), ())), preferred_element_type=F32)


def split2(v):
    high = v.astype(BF16)
    low = (v - high.astype(F32)).astype(BF16)
    return jnp.concatenate([high, low], axis=1)


def sigmoid(v):
    return 0.5 * jnp.tanh(0.5 * v) + 0.5


def silu(v):
    half = 0.5 * v
    return half + half * jnp.tanh(half)


def record_kernel(node_ref, coords_ref, out_ref, parts_ref):
    parts_ref[...] = jnp.zeros_like(parts_ref)
    for a in range(3):
        value = coords_ref[a]
        high = value.astype(BF16).astype(F32)
        rest = value - high
        mid = rest.astype(BF16).astype(F32)
        parts_ref[pl.ds(PIECES + 3 * a, 3), :] = high
        parts_ref[pl.ds(PIECES + 16 + 3 * a, 3), :] = mid
        parts_ref[pl.ds(PIECES + 32 + 3 * a, 3), :] = rest - mid
    eye = (iota((GROUP, GROUP), 0) == iota((GROUP, GROUP), 1)).astype(F32).astype(BF16)
    widen = (iota((64, 128), 0) == iota((64, 128), 1)).astype(F32).astype(BF16)
    record = dot(node_ref[...], widen) + dot_nt(eye, parts_ref[...].astype(BF16))
    out_ref[...] = jnp.broadcast_to(record.astype(BF16)[None], out_ref.shape)


def records(node_state, coords, copies):
    return pl.pallas_call(
        record_kernel,
        out_shape=jax.ShapeDtypeStruct((copies, GROUP, 128), BF16),
        scratch_shapes=[pltpu.VMEM((128, GROUP), F32)],
        name="records",
    )(node_state, coords)


def vmem():
    return pl.BlockSpec(memory_space=pltpu.VMEM)


def in_hbm(v):
    return pltpu.with_memory_space_constraint(v, pltpu.HBM)


def hbm():
    return pl.BlockSpec(memory_space=pltpu.HBM)


def select_kernel(
    lists_hbm,
    pair_ref,
    w_edge_hbm,
    edge_ref,
    pick_col_ref,
    pick_row_ref,
    lists_ref,
    tile_ref,
    rank_ref,
    w_edge_ref,
    w_edge_s,
    sems,
    lists_sem,
    w_edge_sem,
):
    groups = sems.shape[0]

    def fetch(g):
        rows = pl.ds(g * GROUP, GROUP)
        return pltpu.make_async_copy(pair_ref.at[rows], tile_ref.at[rows], sems.at[g])

    lists_copy = pltpu.make_async_copy(lists_hbm, lists_ref, lists_sem)
    lists_copy.start()
    w_edge_copy = pltpu.make_async_copy(w_edge_hbm, w_edge_ref, w_edge_sem)
    w_edge_copy.start()
    start = lax.axis_index("col") * 128
    rows = groups * GROUP
    square = (128, 128)
    before = (iota(square, 0) < iota(square, 1)).astype(F32).astype(BF16)
    eye = (iota(square, 0) == iota(square, 1)).astype(F32).astype(BF16)
    one, other = iota((rows, rows), 0), iota((rows, rows), 1)
    earlier = (lax.shift_right_logical(one, 4) == lax.shift_right_logical(other, 4)) & (one > other)
    earlier = jnp.where(earlier, 1.0, 0.0).astype(BF16)
    lists_copy.wait()
    for g in range(groups):
        fetch(g).start()
    column = iota((128, rows), 0) + start
    chosen = jnp.zeros((128, rows), F32)
    for k in range(K):
        chosen = jnp.where(lists_ref[k : k + 1, :] == column, 1.0, chosen)
    chosen = chosen.astype(BF16)
    totals = dot_t(chosen, jnp.ones(square, BF16)).astype(BF16)
    rank = dot_t(chosen, before) + dot(earlier, totals)
    rank_ref[...] = jnp.where(dot_t(chosen, eye) > 0.0, rank, -1.0)
    slot = iota((SLOTS, 128), 0).astype(F32)
    lane = iota((1, 128), 1)
    w_edge_copy.wait()
    w_edge_s[...] = jnp.zeros_like(w_edge_s)
    w_edge_s[0:64, :] = w_edge_ref[...]

    def group(g, carry):
        fetch(g).wait()
        mark = jnp.zeros((SLOTS, 128), F32)
        picks = []
        ranks = rank_ref[pl.ds(pl.multiple_of(g * GROUP, GROUP), GROUP), :]
        for i in range(GROUP):
            hit = slot == ranks[i : i + 1, :]
            mark = jnp.where(hit, i + 1.0, mark)
            picks.append(jnp.where(hit, 1.0, 0.0).astype(BF16))
        pick = jnp.concatenate(picks, axis=1)
        spots = pl.ds(pl.multiple_of(g * SLOTS, SLOTS), SLOTS)
        tile = tile_ref[pl.ds(pl.multiple_of(g * GROUP, GROUP), GROUP)]
        found = dot(pick, tile.reshape(GROUP * 128, 128)).astype(BF16)
        edge_ref[spots, :] = dot_nt(found, w_edge_s[...])
        pick_col_ref[spots, :] = jnp.where(mark > 0.0, 1.0, 0.0).astype(BF16)
        own = lane - lax.rem(g, GROUPS_PER_STEP) * GROUP
        own = jnp.where((own >= 0) & (own < GROUP), own + 1, -1).astype(F32)
        residue = jnp.sum(mark, axis=1, keepdims=True)
        pick_row_ref[spots, :] = jnp.where(residue == own, 1.0, 0.0).astype(BF16)
        return carry

    lax.fori_loop(0, groups, group, 0, unroll=4)


def select_edges(lists, pair, w_edge):
    groups = pair.shape[0] // GROUP
    shape = (groups * SLOTS, 128)
    return pl.pallas_call(
        select_kernel,
        in_specs=[hbm(), hbm(), hbm()],
        out_specs=[vmem()] * 3,
        out_shape=[jax.ShapeDtypeStruct(shape, dtype) for dtype in (F32, BF16, BF16)],
        scratch_shapes=[
            pltpu.VMEM(lists.shape, jnp.int32),
            pltpu.VMEM(pair.shape, BF16),
            pltpu.VMEM((pair.shape[0], 128), F32),
            pltpu.VMEM(w_edge.shape, BF16),
            pltpu.VMEM((128, 128), BF16),
            pltpu.SemaphoreType.DMA((groups,)),
            pltpu.SemaphoreType.DMA,
            pltpu.SemaphoreType.DMA,
        ],
        compiler_params=pltpu.CompilerParams(vmem_limit_bytes=VMEM_LIMIT),
        cost_estimate=pl.CostEstimate(flops=3_000_000_000, bytes_accessed=9 * 2**20, transcendentals=0),
        name="select_edges",
    )(in_hbm(lists), in_hbm(pair), in_hbm(w_edge))


def edge_kernel(
    edge_ref,
    pick_col_ref,
    pick_row_ref,
    table_ref,
    w_radial_ref,
    w_query_ref,
    w_keyval_ref,
    w_edge_kv_ref,
    w_move_ref,
    out_ref,
    w_keyval_s,
    w_query_s,
    w_radial_s,
    w_mix_s,
    w_move_s,
    rows_ref,
):
    col = lax.axis_index("col")
    for ref in (w_keyval_s, w_query_s, w_radial_s, w_mix_s, w_move_s):
        ref[...] = jnp.zeros_like(ref)
    w_keyval_s[0:64, :] = w_keyval_ref[...]
    w_query_s[0:64, 0:64] = (-w_query_ref[...].astype(F32)).astype(BF16)
    w_radial_s[0:36, 0:64] = w_radial_ref[...].astype(F32)
    w_radial = w_radial_s[...].astype(BF16)
    w_mix_s[0:64, 0:128] = w_edge_kv_ref[...]
    w_move_s[0:12, 0:64] = w_move_ref[...].astype(F32)
    w_mix_s[:, 128:256] = jnp.transpose(w_move_s[...]).astype(BF16)
    rows = table_ref[pl.ds(pl.multiple_of(lax.axis_index("row") * 256, 256), 256), :]
    rows_ref[...] = rows
    cols = table_ref[pl.ds(pl.multiple_of(col * 128, 128), 128), :]
    keyval = dot(cols, w_keyval_s[...]).astype(BF16)
    lane = iota((1, 128), 1)
    cols = jnp.where(lane < PIECES, 0.0, cols.astype(F32)).astype(BF16)
    by_column = jnp.concatenate([keyval, cols], axis=1)
    source = iota((256, 256), 0)
    target = iota((256, 256), 1)
    channel = jnp.bitwise_and(source, 127)
    head = lax.shift_right_logical(channel, 4)
    for_value = (target >= 64) & (target < 128) & (lax.shift_right_logical(target - 64, 4) == head)
    for_move = (target >= 128) & (target < 140) & (jnp.bitwise_and(target, 3) == head)
    heads = jnp.where((channel < 64) & (for_value | for_move), 0.125, 0.0).astype(BF16)
    source = jnp.bitwise_and(iota((256, 128), 0), 127)
    target = iota((256, 128), 1) - PIECES
    low_atom = lax.shift_right_logical(source, 2) * 3
    spread = jnp.where(
        (source < 12) & (target >= low_atom) & (target < low_atom + 3), 1.0, 0.0
    ).astype(BF16)
    centre = lane.astype(F32) * CENTRE_STEP
    alpha = jnp.where((lane >= PIECES + 3) & (lane < PIECES + 6), 1.0, 0.0)
    per = GROUPS_PER_STEP * SLOTS
    own = GROUPS_PER_STEP * GROUP
    steps = edge_ref.shape[0] // per
    parts = []
    for step in range(steps):
        spots = pl.ds(step * per, per)
        pick_col = pick_col_ref[spots, :]
        pick_row = pick_row_ref[spots, :]
        rows = rows_ref[pl.ds(step * own, own), :]
        by_row = jnp.concatenate([jnp.zeros_like(rows), (-rows.astype(F32)).astype(BF16)], axis=1)
        picked = dot(
            jnp.concatenate([pick_col, pick_row], axis=1), jnp.concatenate([by_column, by_row], axis=0)
        )
        gap = picked[:, 128:]
        relative = gap + pltpu.roll(gap, 112, 1) + pltpu.roll(gap, 96, 1)
        distance = jnp.sqrt(jnp.sum(relative * relative * alpha, axis=1, keepdims=True))
        offset = (distance - centre) * 2.0
        basis = jnp.exp(-(offset * offset)).astype(BF16)
        hidden = silu(edge_ref[spots, :] + dot(basis, w_radial)).astype(BF16)
        mix = dot(hidden, w_mix_s[...])
        keyval_edge = picked[:, :128] + mix[:, :128]
        queries = dot(gap.astype(BF16), w_query_s[...])
        attention = 0.5 * jnp.tanh(dot(split2(queries * keyval_edge), heads)) + 0.5
        values = attention[:, :128] * keyval_edge
        moves = attention[:, 128:] * mix[:, 128:]
        move = dot(split2(moves), spread) * relative
        both = jnp.where(lane < 64, pltpu.roll(move, 64, 1), values)
        summed = dot_t(pick_row, split2(both))
        parts.append((summed[:own, :128] + summed[:own, 128:]) * (1.0 / K))
    total = jnp.concatenate(parts, axis=0)
    atoms = rows_ref[...].astype(F32)
    atoms = atoms + pltpu.roll(atoms, 112, 1) + pltpu.roll(atoms, 96, 1)
    first = jnp.where(col == 0, 1.0, 0.0)
    total = total + jnp.where(lane < 9, pltpu.roll(atoms, 64, 1), 0.0) * first
    by_lane = jnp.transpose(total)
    groups = out_ref.shape[0]
    for d in range(groups):
        out_ref[d, 0:16, :] = total[d * GROUP : (d + 1) * GROUP, :]
        out_ref[d, 16:24, :] = by_lane[0:8, 0:128]
        out_ref[d, 24:32, :] = by_lane[0:8, 128:256]
        out_ref[d, 32:40, :] = jnp.concatenate(
            [by_lane[8:9, 0:128], by_lane[8:9, 128:256], jnp.zeros((6, 128), F32)], axis=0
        )


def edge_sums(edge, pick_col, pick_row, table, w_radial, w_query, w_keyval, w_edge_kv, w_move):
    groups = edge.shape[0] // SLOTS
    operands = (edge, pick_col, pick_row, table, w_radial, w_query, w_keyval, w_edge_kv, w_move)
    whole = lambda shape: pl.BlockSpec(shape, lambda i: (0,) * len(shape))
    return pl.pallas_call(
        edge_kernel,
        grid=(1,),
        in_specs=[vmem()] * 4 + [whole(a.shape) for a in operands[4:]],
        out_specs=whole((groups, 40, 128)),
        scratch_shapes=[pltpu.VMEM((128, 128), BF16)] * 2
        + [
            pltpu.VMEM((128, 128), F32),
            pltpu.VMEM((128, 256), BF16),
            pltpu.VMEM((128, 128), F32),
            pltpu.VMEM((groups * GROUP, 128), BF16),
        ],
        out_shape=jax.ShapeDtypeStruct((groups, 40, 128), F32),
        compiler_params=pltpu.CompilerParams(vmem_limit_bytes=VMEM_LIMIT),
        cost_estimate=pl.CostEstimate(flops=2_000_000_000, bytes_accessed=3 * 2**20, transcendentals=0),
        name="edge_sums",
    )(*operands)


def total_kernel(parts_ref, node_ref, w_out_ref, node_out_ref, own_ref, rows_ref, send_ref, w_ref):
    col = lax.axis_index("col")
    total = parts_ref[0]
    for d in range(1, parts_ref.shape[0]):
        total = total + parts_ref[d]
    w_ref[...] = jnp.zeros_like(w_ref)
    w_ref[64:128, :] = w_out_ref[...]
    message = total[0:16, :].astype(BF16)
    node_out_ref[...] = node_ref[...].astype(F32) + dot(message, w_ref[...])
    left = jnp.concatenate([total[16:24, :], total[32:33, :], jnp.zeros((7, 128), F32)], axis=0)
    right = jnp.concatenate([total[24:32, :], total[33:34, :], jnp.zeros((7, 128), F32)], axis=0)
    rows_ref[:, 0:128] = left
    rows_ref[:, 128:256] = right
    odd = jnp.bitwise_and(col, 1) == 1
    send_ref[...] = jnp.broadcast_to(jnp.where(odd, right, left)[None], send_ref.shape)
    mine = jnp.where(col >= 8, right, left)
    mine = pltpu.roll(mine, jnp.bitwise_and(128 - jnp.bitwise_and(col, 7) * GROUP, 127), 1)
    for a in range(3):
        own_ref[a] = mine[3 * a : 3 * a + 3, 0:GROUP]


def totals(parts, node_state, w_out, copies):
    operands = (parts, node_state, w_out)
    shapes = ((GROUP, 64), (3, 3, GROUP), (16, 256), (copies, 16, 128))
    whole = lambda shape: pl.BlockSpec(shape, lambda i: (0,) * len(shape))
    return pl.pallas_call(
        total_kernel,
        grid=(1,),
        in_specs=[whole(a.shape) for a in operands],
        out_specs=[whole(shape) for shape in shapes],
        out_shape=[jax.ShapeDtypeStruct(shape, F32) for shape in shapes],
        scratch_shapes=[pltpu.VMEM((128, 64), BF16)],
        compiler_params=pltpu.CompilerParams(vmem_limit_bytes=SMALL_LIMIT),
        name="totals",
    )(*operands)


def transition_step(x, w_in, w_out, half_gate):
    x = x.astype(F32)
    centred = x - jnp.mean(x, axis=1, keepdims=True)
    mean = jnp.full((128, 128), 1.0 / 128.0, BF16)
    scale = lax.rsqrt(dot((centred * centred).astype(BF16), mean) + 1e-05)
    normed = (centred * scale).astype(BF16)
    hidden = jnp.maximum(dot(normed, w_in).astype(BF16), 0)
    return x + dot(hidden, w_out), jnp.tanh(dot(normed, half_gate)) + 1.0


def halved(ref):
    return (ref[...].astype(F32) * 0.5).astype(BF16)


def transition_kernel(first, pair_ref, w_in_ref, w_out_ref, w_gate_ref, base_ref, gate_ref, x_s, *refs):
    base_s, gate_s = refs[:2] if len(refs) == 4 else (base_ref, gate_ref)
    sems, sem = refs[-2:]
    count = x_s.shape[0]

    def fetch(n):
        rows = pl.ds(n * BLOCK, BLOCK)
        return pltpu.make_async_copy(pair_ref.at[pl.ds(first + n * BLOCK, BLOCK)], x_s.at[rows], sems.at[n])

    for n in range(count // BLOCK):
        fetch(n).start()
    half_gate = halved(w_gate_ref)

    def step(n, carry):
        fetch(n).wait()
        for i in range(0, BLOCK, STEP):
            rows = pl.ds(n * BLOCK + i, STEP)
            x = x_s[rows].reshape(STEP * 128, 128)
            base, gate = transition_step(x, w_in_ref[...], w_out_ref[...], half_gate)
            base_s[rows] = base.astype(BF16).reshape(STEP, 128, 128)
            gate_s[rows] = gate.astype(BF16).reshape(STEP, 128, 128)
        if base_s is not base_ref:
            rows = pl.ds(n * BLOCK, BLOCK)
            pltpu.make_async_copy(base_s.at[rows], base_ref.at[rows], sem).start()
            pltpu.make_async_copy(gate_s.at[rows], gate_ref.at[rows], sem).start()
        return carry

    lax.fori_loop(0, count // BLOCK, step, 0)
    if base_s is not base_ref:
        pltpu.make_async_copy(base_s, base_ref, sem).wait()
        pltpu.make_async_copy(gate_s, gate_ref, sem).wait()


def transition(pair, w_in, w_out, w_gate, first, count, keep=False):
    shape = (count,) + pair.shape[1:]
    return pl.pallas_call(
        functools.partial(transition_kernel, first),
        in_specs=[hbm()] + [vmem()] * 3,
        out_specs=[vmem() if keep else hbm()] * 2,
        out_shape=[(pltpu.VMEM if keep else pltpu.HBM)(shape, BF16)] * 2,
        scratch_shapes=[pltpu.VMEM(shape, BF16)] * (1 if keep else 3)
        + [pltpu.SemaphoreType.DMA((count // BLOCK,)), pltpu.SemaphoreType.DMA],
        compiler_params=pltpu.CompilerParams(vmem_limit_bytes=VMEM_LIMIT),
        cost_estimate=pl.CostEstimate(
            flops=count * 128 * 2 * 128 * 640, bytes_accessed=count * 128 * 128 * 6, transcendentals=0
        ),
        name="transition",
    )(in_hbm(pair), w_in, w_out, w_gate)


def structure_kernel(
    counts, rows_ref, chain_ref, cols_ref, chains_ref, w_in_ref, w_out_ref, w_up_ref, w_down_ref, w_gate_ref, pair_ref, *refs
):
    held = refs[: 2 * len(counts)]
    out_ref, base_s, gate_s, made_s, w_in_f, w_in_s, w_out_s, sems, sem = refs[2 * len(counts) :]
    done = sum(counts)
    total = base_s.shape[0]
    blocks = total // BLOCK

    def fetch(n):
        at = n * BLOCK
        rows = pl.ds(at, BLOCK)
        if at >= done:
            return [pltpu.make_async_copy(pair_ref.at[rows], base_s.at[rows], sems.at[n])]
        part = 0
        while at >= counts[part]:
            at -= counts[part]
            part += 1
        if part == len(counts) - 1:
            return []
        source = pl.ds(at, BLOCK)
        return [
            pltpu.make_async_copy(held[2 * part].at[source], base_s.at[rows], sems.at[n]),
            pltpu.make_async_copy(held[2 * part + 1].at[source], gate_s.at[rows], sems.at[blocks + n]),
        ]

    for n in range(blocks):
        for copy in fetch(n):
            copy.start()
    row_index = lax.axis_index("row")
    col_index = lax.axis_index("col")
    w_in_f[...] = jnp.zeros_like(w_in_f)
    w_out_s[...] = jnp.zeros_like(w_out_s)
    half = w_in_ref[...].astype(F32) * 0.5
    for k in range(2):
        w_in_f[48 * k : 48 * k + 36, 128 * k : 128 * (k + 1)] = half[0:36]
        w_in_f[48 * k + 40 : 48 * k + 46, 128 * k : 128 * (k + 1)] = half[36:42]
        w_out_s[128 * k : 128 * (k + 1), 128 * k : 128 * (k + 1)] = halved(w_out_ref)
    w_in_s[...] = w_in_f[...].astype(BF16)
    half_gate = halved(w_gate_ref)

    cols = cols_ref[lax.shift_right_logical(col_index, 1)]
    wide = lambda v: jnp.broadcast_to(v, (8, 128))
    alpha = [wide(cols[3 + x : 4 + x, :]) for x in range(3)]
    feature = iota((8, 128), 0)
    bonds = [
        jnp.where(
            feature == 2,
            alpha[x] - wide(cols[x : x + 1, :]),
            jnp.where(feature == 3, alpha[x] - wide(cols[6 + x : 7 + x, :]), 0.0),
        )
        for x in range(3)
    ]
    chain = wide(chains_ref[pl.ds(col_index, 1), :])
    position = iota((8, 128), 1) + col_index * 128
    centre = [(iota((8, 128), 0) + 8 * b).astype(F32) * CENTRE_STEP for b in range(5)]

    def features(row):
        p = [rows_ref[3 + x, row] for x in range(3)]
        rn = [rows_ref[x, row] - p[x] for x in range(3)]
        rc = [rows_ref[6 + x, row] - p[x] for x in range(3)]
        gap = [alpha[x] - p[x] for x in range(3)]
        square = gap[0] * gap[0] + gap[1] * gap[1] + gap[2] * gap[2]
        distance = jnp.sqrt(square)
        inverse = 1.0 / (1.0 + distance)
        vectors = [
            jnp.where(feature == 0, rn[x], jnp.where(feature == 1, rc[x], bonds[x])) for x in range(3)
        ]
        orient = (vectors[0] * gap[0] + vectors[1] * gap[1] + vectors[2] * gap[2]) * inverse
        at = row + row_index * 256
        same = jnp.where(chain == chain_ref[at], 1.0, 0.0)
        offset = same * (jnp.clip(position - at, -32, 32).astype(F32) * (1.0 / 32.0))
        tail = jnp.where(feature == 4, same, jnp.where(feature == 5, offset, orient))
        tail = jnp.where(feature < 6, tail, 0.0)
        basis = []
        for b in range(5):
            t = (distance - centre[b]) * 2.0
            basis.append(jnp.exp(-(t * t)))
        return basis + [tail]

    def terms(start, per):
        feats = []
        for u in range(per // 2):
            row = start + 2 * u
            feats.append(jnp.concatenate(features(row) + features(row + 1), axis=0).astype(BF16))
        half = dot_t(jnp.concatenate(feats, axis=1), w_in_s[...])
        hidden = (half + half * jnp.tanh(half)).astype(BF16)
        term = dot(hidden, w_out_s[...])
        return [
            term[128 * (u // 2) : 128 * (u // 2 + 1), 128 * (u % 2) : 128 * (u % 2 + 1)] for u in range(per)
        ]

    def finish_held(start, base_ref=base_s, gate_ref=gate_s, first=0):
        for u, term in enumerate(terms(start, HELD_STEP)):
            gate = gate_ref[start - first + u].astype(F32)
            made_s[start + u] = (base_ref[start - first + u].astype(F32) + gate * term).astype(BF16)

    def finish_whole(start):
        term = terms(start, STEP)
        x = base_s[pl.ds(start, STEP)].reshape(STEP * 128, 128)
        base, gate = transition_step(x, w_up_ref[...], w_down_ref[...], half_gate)
        for u in range(STEP):
            spot = slice(128 * u, 128 * (u + 1))
            made_s[start + u] = (base[spot] + gate[spot] * term[u]).astype(BF16)

    def send(n):
        rows = pl.ds(n * BLOCK, BLOCK)
        pltpu.make_async_copy(made_s.at[rows], out_ref.at[rows], sem).start()

    def await_block(n, pair_too):
        rows = pl.ds(n * BLOCK, BLOCK)
        pltpu.make_async_copy(pair_ref.at[rows], base_s.at[rows], sems.at[n]).wait()
        if pair_too:
            pltpu.make_async_copy(pair_ref.at[rows], gate_s.at[rows], sems.at[blocks + n]).wait()

    def step(finish, copies, per, n, carry):
        if copies:
            await_block(n, copies == 2)
        for i in range(0, BLOCK, per):
            finish(n * BLOCK + i)
        send(n)
        return carry

    copied = done - counts[-1]
    finish_kept = functools.partial(
        finish_held, base_ref=held[-2], gate_ref=held[-1], first=copied
    )
    kept_step = functools.partial(step, finish_kept, 0, HELD_STEP)
    lax.fori_loop(copied // BLOCK, done // BLOCK, kept_step, 0)
    lax.fori_loop(0, copied // BLOCK, functools.partial(step, finish_held, 2, HELD_STEP), 0)
    lax.fori_loop(done // BLOCK, blocks, functools.partial(step, finish_whole, 1, STEP), 0)
    pltpu.make_async_copy(made_s, out_ref, sem).wait()


def structure(rows, chain, cols, w_in, w_out, w_up, w_down, w_gate, pair, held):
    smem = pl.BlockSpec(memory_space=pltpu.SMEM)
    counts = tuple(base.shape[0] for base in held[0::2])
    blocks = pair.shape[0] // BLOCK
    return pl.pallas_call(
        functools.partial(structure_kernel, counts),
        in_specs=[smem, smem] + [vmem()] * 7 + [hbm()] * (len(held) - 1) + [vmem()] * 2,
        out_specs=hbm(),
        scratch_shapes=[pltpu.VMEM(pair.shape, BF16)] * 3
        + [
            pltpu.VMEM((96, 256), F32),
            pltpu.VMEM((96, 256), BF16),
            pltpu.VMEM((256, 256), BF16),
            pltpu.SemaphoreType.DMA((2 * blocks,)),
            pltpu.SemaphoreType.DMA,
        ],
        out_shape=jax.ShapeDtypeStruct(pair.shape, BF16),
        compiler_params=pltpu.CompilerParams(vmem_limit_bytes=VMEM_LIMIT),
        name="structure",
    )(rows, chain, cols, chain.reshape(-1, 128), w_in, w_out, w_up, w_down, w_gate, in_hbm(pair), *map(in_hbm, held[:-2]), *held[-2:])


def exchange(v, axis):
    return lax.all_to_all(v, axis, split_axis=0, concat_axis=0, tiled=True)


def local(
    pair,
    node_state,
    coords,
    neighbours,
    chain,
    w_edge,
    w_radial,
    w_query,
    w_keyval,
    w_edge_kv,
    w_out,
    w_move,
    w_trans_in,
    w_trans_out,
    w_gate,
    w_feat_in,
    w_feat_out,
):
    row_devices = lax.axis_size("row")
    col_devices = lax.axis_size("col")
    step = functools.partial(transition, w_in=w_trans_in, w_out=w_trans_out, w_gate=w_gate)

    table = exchange(records(node_state, coords, row_devices * col_devices), BOTH)
    edge, pick_col, pick_row = select_edges(neighbours.T, pair, w_edge.T)
    pair, edge = lax.optimization_barrier((pair, edge))
    held = step(pair, first=0, count=PARTS[0]) if PARTS[0] else []
    parts = edge_sums(
        edge,
        pick_col,
        pick_row,
        table.reshape(-1, 128),
        w_radial,
        w_query,
        w_keyval,
        w_edge_kv,
        w_move.T,
    )
    pair, parts, held = lax.optimization_barrier((pair, parts, held))
    parts = exchange(parts, "col")
    held += step(pair, first=PARTS[0], count=PARTS[1])
    node_out, own, rows, send = totals(parts, node_state, w_out, row_devices)
    pair, send, held = lax.optimization_barrier((pair, send, held))
    cols = exchange(send, "row")
    held += step(pair, first=PARTS[0] + PARTS[1], count=PARTS[2], keep=True)
    pair_out = structure(
        rows, chain, cols, w_feat_in, w_feat_out, w_trans_in, w_trans_out, w_gate, pair, held
    )
    return (pair_out, node_out, own)


def solution(mesh):
    spread = P(None, None, BOTH)
    in_specs = (P("row", "col", None), P(BOTH, None), spread, P("row", None)) + (P(),) * 13
    out_specs = (P("row", "col", None), P(BOTH, None), spread)
    return jax.shard_map(local, mesh=mesh, in_specs=in_specs, out_specs=out_specs, check_vma=False)
```
